256 devices in a mesh: rep: 64 (over z_hi, y, x), tp: 4 (over z_lo, core).
Axes of the slice: x: 4, y: 4, z: 8 (z_hi: 4, z_lo: 2; z = z_hi * 2 + z_lo), core: 2. Of those that a mesh axis runs over, the one named last changes fastest.
Arguments:
- attn_out: bfloat16 [64, 512, 2048], P('rep', None, 'tp'), may hold values from -6 to 6
- proj_weight: bfloat16 [64, 2048, 4608], P('rep', 'tp'), may hold values from -0.125 to 0.125
- norm_gain: float32 [64, 4608], P('rep'), may hold values from 0.5 to 1.5
- cotangent: bfloat16 [64, 512, 4608], P('rep', 'tp'), may hold values from -3 to 3
- coeffs: float32 [64, 4, 48, 64, 64], P('rep', 'tp'), may hold values from -192 to 192
- tile_ids: int32 [64, 4, 48], P('rep', 'tp'), may hold values from 0 to 511, as said below
- tiles: float32 [4, 512, 64, 64], P('tp', 'rep'), may hold values from -6 to 6
- momentum: float32 [4, 512, 64, 64], P('tp', 'rep'), may hold values from -3 to 3
Outputs:
- weight_grad: bfloat16 [64, 2048, 4608], P('rep', 'tp')
- input_grad: bfloat16 [64, 512, 2048], P('rep', None, 'tp')
- tiles_new: float32 [4, 512, 64, 64], P('tp', 'rep')
- momentum_new: float32 [4, 512, 64, 64], P('tp', 'rep')
The draws below stay inside these ranges and needn't reach their ends.
Inputs may be any that keep to these rules, and one draw needn't show every extreme that they name: The owner of tile i is i // 8. For each replica r and group t, at most 2 entries of tile_ids[r, t, :] name tiles of one owner; in every group some owner is named exactly 2 times by every replica.
All inputs are finite; a program needn't handle non-finite values.
Results may differ from the reference program's by a relative error of at most 0.0095.
Values may be sent and summed in bfloat16 or wider, within the bound.
A program may use at most 128 MiB of HBM per device.

```python
import jax
import jax.numpy as jnp
from jax import lax

D = 4608
TILE = 64
OWN = 8
TOK = 512
HD = 2048
REPS = 64
TPS = 4
NT_G = 512
K_DEV = 48
N_REP = 64


def draw_tile_ids(key, part):
    key = jax.random.fold_in(key, 7)

    def group_draw(group_key, group):
        key_hot, key_rest = jax.random.split(group_key, 2)
        chosen = jax.random.randint(key_hot, (), 0, N_REP).astype(jnp.int32)
        hot_owner = jnp.where(group == 0, N_REP - 1, jnp.where(group == 1, 0, chosen)).astype(jnp.int32)
        owner_pool = (jnp.arange(2 * (N_REP - 1), dtype=jnp.int32) // 2).astype(jnp.int32)
        owner_pool = (owner_pool + (owner_pool >= hot_owner).astype(jnp.int32)).astype(jnp.int32)
        hot_names = (jnp.array([0, OWN - 1], dtype=jnp.int32) + hot_owner * OWN).astype(jnp.int32)

        def replica_draw(replica_key):
            key_pick, key_offset, key_mixed = jax.random.split(replica_key, 3)
            picked = jax.random.permutation(key_pick, owner_pool)[:K_DEV - 2]
            offsets = jax.random.randint(key_offset, (K_DEV - 2,), 0, OWN).astype(jnp.int32)
            joined = jnp.concatenate([hot_names, (picked * OWN + offsets).astype(jnp.int32)])
            return jax.random.permutation(key_mixed, joined).astype(jnp.int32)
        return jax.vmap(replica_draw)(jax.random.split(key_rest, N_REP))
    groups = jax.vmap(group_draw)(jax.random.split(key, TPS), jnp.arange(TPS, dtype=jnp.int32))
    return jnp.transpose(groups, (1, 0, 2)).astype(jnp.int32)


def level_of(own_key, extent, shards, least, high):
    factor_of = 1.0
    for dim, shards_of in shards:
        heights = jax.random.uniform(jax.random.fold_in(jax.random.fold_in(own_key, 6), dim), (shards_of,), jnp.float32, least / len(shards), high / len(shards))
        factor_of = factor_of * jnp.repeat(jnp.exp(heights), extent[dim] // shards_of).reshape((-1,) + (1,) * (len(extent) - 1 - dim))
    return factor_of


def gaussian(own_key, extent, deviation, bound, pieces=(), held_as=jnp.bfloat16):
    factor_of = level_of(own_key, extent, pieces, -0.22, 0.18) if pieces else 1.0
    values = jax.random.normal(own_key, extent, jnp.float32) * deviation * factor_of
    return jnp.minimum(jnp.maximum(values, -bound), bound).astype(held_as)


def setup_inputs(seed: int = 0) -> dict:
    seeds = jax.random.split(jax.random.key(seed), 9)
    attn_out = gaussian(seeds[0], (REPS, TOK, HD), 1.0, 6.0, ((0, 64), (2, 4)))
    proj_weight = gaussian(seeds[1], (REPS, HD, D), HD ** -0.5, 0.125, ((0, 64), (1, 4)))
    norm_gain = jnp.clip(1.0 + 0.1 * jax.random.normal(seeds[2], (REPS, D), jnp.float32), 0.5, 1.5)
    cotangent = gaussian(seeds[3], (REPS, TOK, D), (TOK ** -0.25), 3.0, ((0, 64), (1, 4)))
    coeffs = gaussian(seeds[4], (REPS, TPS, K_DEV, TILE, TILE), (REPS * 0.5), 192.0, ((0, 64), (1, 4)), jnp.float32)
    tile_ids = draw_tile_ids(jax.random.fold_in(seeds[8], 71), 0)
    tiles = gaussian(seeds[6], (TPS, NT_G, TILE, TILE), 1.0, 6.0, ((0, 4), (1, 64)), jnp.float32)
    momentum = gaussian(seeds[7], (TPS, NT_G, TILE, TILE), 0.5, 3.0, ((0, 4), (1, 64)), jnp.float32)
    return {"attn_out": attn_out, "proj_weight": proj_weight, "norm_gain": norm_gain, "cotangent": cotangent, "coeffs": coeffs, "tile_ids": tile_ids, "tiles": tiles, "momentum": momentum}


eps = 1e-06
outer_rate = 0.7
momentum_decay = 0.9

def norm_back(projected, upstream, norm_scale):
    inverse_rms = lax.rsqrt(lax.optimization_barrier(jnp.mean(projected * projected, axis=-1, keepdims=True)) + eps)
    normed = projected * inverse_rms
    scaled = upstream * norm_scale
    return (inverse_rms * (scaled - normed * lax.optimization_barrier(jnp.mean(scaled * normed, axis=-1, keepdims=True)))).astype(jnp.bfloat16)

def dct_basis(size):
    freq = jnp.arange(size, dtype=jnp.float32)[:, None]
    place = jnp.arange(size, dtype=jnp.float32)[None, :]
    scales = jnp.where(freq == 0, jnp.sqrt(1.0 / size), jnp.sqrt(2.0 / size))
    return scales * jnp.cos(jnp.pi * (2.0 * place + 1.0) * freq / (2.0 * size))

def decode(coef_tiles, basis):
    right = jnp.einsum('jkl,lb->jkb', coef_tiles, basis, precision=lax.Precision.HIGHEST)
    return jnp.einsum('ka,jkb->jab', basis, right, precision=lax.Precision.HIGHEST)

def replica_step(operands):
    attended, weights, norm_scale, upstream = operands
    width = weights.shape[0] // TPS
    projected = jnp.zeros((attended.shape[0], weights.shape[1]), jnp.float32)
    for column in range(TPS):
        part_sum = jnp.dot(attended[:, column * width:(column + 1) * width], weights[column * width:(column + 1) * width], preferred_element_type=jnp.float32)
        rounded = lax.optimization_barrier(part_sum.astype(jnp.bfloat16))
        projected = projected + rounded.astype(jnp.float32)
    grad_out = norm_back(projected, upstream.astype(jnp.float32), norm_scale)
    weight_part = lax.dot_general(attended, grad_out, (((0,), (0,)), ((), ())), preferred_element_type=jnp.float32).astype(jnp.bfloat16)
    input_part = lax.dot_general(grad_out, weights, (((1,), (1,)), ((), ())), preferred_element_type=jnp.float32).astype(jnp.bfloat16)
    return (weight_part, input_part)

def reference(attn_out, proj_weight, norm_gain, cotangent, coeffs, tile_ids, tiles, momentum):
    weight_grad, input_grad = lax.map(replica_step, (attn_out, proj_weight, norm_gain, cotangent))
    tile_area = TILE * TILE
    offsets = (jnp.arange(TPS, dtype=jnp.int32) * NT_G)[None, :, None]
    segment_ids = (tile_ids + offsets).reshape(-1).astype(jnp.int32)
    coef_sums = jax.ops.segment_sum(coeffs.reshape(-1, tile_area), segment_ids, num_segments=TPS * NT_G)
    coef_tiles = coef_sums.reshape(TPS * NT_G, TILE, TILE)
    decoded = decode(coef_tiles, dct_basis(TILE)).reshape(TPS, NT_G, TILE, TILE) / REPS
    momentum_new = momentum_decay * momentum + decoded
    tiles_new = tiles - outer_rate * (decoded + momentum_decay * momentum_new)
    return (weight_grad, input_grad, tiles_new, momentum_new)
```

```python
import jax
import jax.numpy as jnp
import numpy as np
from jax import lax
from jax.experimental import pallas as pl
from jax.experimental.pallas import tpu as pltpu
from jax.sharding import PartitionSpec as P

eps = 1e-06
outer_rate = 0.7
momentum_decay = 0.9
MESH = pl.DeviceIdType.MESH
PLANES = 4
PARTS = 4
ROW_CHUNKS = (32, 32, 32, 32)
HEAD = 16


def dct_basis(size):
    freq = np.arange(size, dtype=np.float64)[:, None]
    place = np.arange(size, dtype=np.float64)[None, :]
    scales = np.where(freq == 0, np.sqrt(1.0 / size), np.sqrt(2.0 / size))
    return (scales * np.cos(np.pi * (2.0 * place + 1.0) * freq / (2.0 * size))).astype(np.float32)


def owner_table(names, owners, owned):
    entry = jnp.arange(names.shape[0], dtype=jnp.int32)[None, :]
    match = (names // owned)[None, :] == jnp.arange(owners, dtype=jnp.int32)[:, None]
    place = (names % owned)[None, :]
    first = jnp.min(jnp.where(match, entry, names.shape[0]), axis=1)
    last = jnp.max(jnp.where(match, entry, -1), axis=1)
    first_place = jnp.max(jnp.where(match & (entry == first[:, None]), place, -1), axis=1)
    last_place = jnp.max(
        jnp.where(match & (entry == last[:, None]) & (entry > first[:, None]), place, -1), axis=1
    )
    first = jnp.where(first_place >= 0, first, 0)
    last = jnp.maximum(last, 0)
    return jnp.stack([first, last, first_place, last_place])


def step_kernel(
    table, attn_hbm, w_hbm, gain_hbm, ct_hbm, coef_hbm, tiles_hbm, mom_hbm, left_hbm, right_hbm,
    wg_hbm, ig_hbm, tiles_out, mom_out,
    attn, attn_t, w, gain, ct, coef, tiles, mom, left, right,
    part, sib_part, pair_sum, far_sum, proj, grad, acc, wg, ig,
    pack, packs_in, sums, sums_out, sums_in, tiles_new, mom_new,
    in_sem, w_sem, attn_sem, out_sem, wg_sem, ig_sem,
    core_s, core_r, z_s, z_r, gz_s, gz_r, gc_s, gc_r, gf_s, gf_r,
    pa_s, pa_r, pb_s, pb_r,
):
    n_rep = lax.axis_size("rep")
    planes = PLANES
    n_xy = n_rep // planes
    rep, tp = lax.axis_index("rep"), lax.axis_index("tp")
    xy, zh = lax.rem(rep, n_xy), lax.div(rep, n_xy)
    core, zl = lax.rem(tp, 2), lax.div(tp, 2)
    sib = zl * 2 + 1 - core
    far = (1 - zl) * 2 + core
    diag = (1 - zl) * 2 + 1 - core
    order = (tp, far, sib, diag)
    depth = w.shape[0]
    width = w.shape[1]
    rows = ct.shape[0]
    tile_w = w_sem_width(width)
    n_w = width // tile_w
    side = coef.shape[1]
    chunks = []
    off = 0
    for size in ROW_CHUNKS:
        chunks.append((off, size))
        off += size
    f32, bf16 = jnp.float32, jnp.bfloat16

    def xy_peer(d):
        return zh * n_xy + lax.rem(xy + d, n_xy)

    def zh_peer(e):
        return lax.rem(zh + e, planes) * n_xy + xy

    loads = []
    for j, (o, s) in enumerate(chunks):
        for p in range(PARTS):
            start = pl.multiple_of(order[p] * rows + o, 16)
            copy = pltpu.make_async_copy(
                attn_hbm.at[pl.ds(start, s)],
                attn.at[pl.ds(4 * o + p * s, s)],
                attn_sem.at[j * PARTS + p],
            )
            copy.start()
            loads.append(copy)
    w_loads = []
    for n in range(n_w):
        cols = pl.ds(n * tile_w, tile_w)
        copy = pltpu.make_async_copy(w_hbm.at[:, cols], w.at[:, cols], w_sem.at[n])
        copy.start()
        w_loads.append(copy)
    others = []
    for i, (src, dst) in enumerate(
        ((coef_hbm, coef), (ct_hbm, ct), (gain_hbm, gain), (tiles_hbm, tiles), (mom_hbm, mom),
         (left_hbm, left), (right_hbm, right))
    ):
        copy = pltpu.make_async_copy(src, dst, in_sem.at[i])
        copy.start()
        others.append(copy)
    coef_load, ct_load, gain_load, tiles_load, mom_load, left_load, right_load = others

    barrier = pltpu.get_barrier_semaphore()
    pl.semaphore_signal(barrier, inc=1, device_id=(rep, sib), device_id_type=MESH)
    pl.semaphore_signal(barrier, inc=1, device_id=(rep, far), device_id_type=MESH)

    @pl.loop(1, n_xy)
    def _(d):
        pl.semaphore_signal(barrier, inc=1, device_id=(xy_peer(d), tp), device_id_type=MESH)

    @pl.loop(1, planes)
    def _(e):
        pl.semaphore_signal(barrier, inc=1, device_id=(zh_peer(e), tp), device_id_type=MESH)

    def partial_chunk(j):
        o, s = chunks[j]
        block = attn[4 * o:4 * o + 4 * s, :]

        @pl.loop(0, n_w)
        def _(n):
            cols = pl.ds(pl.multiple_of(n * tile_w, tile_w), tile_w)
            if j == 0:
                pltpu.make_async_copy(w_hbm.at[:, cols], w.at[:, cols], w_sem.at[n]).wait()
            part[4 * o:4 * o + 4 * s, cols] = jnp.dot(
                block, w[:, cols], preferred_element_type=f32
            ).astype(bf16)

    def remote(src, dst, send, recv, rep_to, tp_to):
        return pltpu.make_async_remote_copy(
            src_ref=src, dst_ref=dst, send_sem=send, recv_sem=recv,
            device_id=(rep_to, tp_to), device_id_type=MESH,
        )

    def core_copy(j):
        o, s = chunks[j]
        return remote(
            part.at[pl.ds(4 * o + 2 * s, 2 * s)], sib_part.at[pl.ds(2 * o, 2 * s)],
            core_s.at[j], core_r.at[j], rep, sib,
        )

    def z_copy(j):
        o, s = chunks[j]
        return remote(
            pair_sum.at[pl.ds(o, s)], far_sum.at[pl.ds(o, s)], z_s.at[j], z_r.at[j], rep, far
        )

    def grad_far(j):
        o, s = chunks[j]
        return remote(
            grad.at[pl.ds(4 * o, s)], grad.at[pl.ds(4 * o + s, s)], gz_s.at[j], gz_r.at[j], rep, far
        )

    def grad_core(j):
        o, s = chunks[j]
        return remote(
            grad.at[pl.ds(4 * o, s)], grad.at[pl.ds(4 * o + 2 * s, s)],
            gc_s.at[j], gc_r.at[j], rep, sib,
        )

    def grad_forward(j):
        o, s = chunks[j]
        return remote(
            grad.at[pl.ds(4 * o + s, s)], grad.at[pl.ds(4 * o + 3 * s, s)],
            gf_s.at[j], gf_r.at[j], rep, sib,
        )

    def pair_chunk(j):
        o, s = chunks[j]
        core_copy(j).wait_recv()

        @pl.loop(0, n_w)
        def _(n):
            cols = pl.ds(pl.multiple_of(n * tile_w, tile_w), tile_w)
            pair_sum[o:o + s, cols] = (
                part[4 * o + s:4 * o + 2 * s, cols].astype(f32)
                + sib_part[2 * o + s:2 * o + 2 * s, cols].astype(f32)
            ).astype(bf16)

        z_copy(j).start()

    def fold(block):
        total = block[:, 0:128]
        for k in range(1, block.shape[1] // 128):
            total = total + block[:, k * 128:(k + 1) * 128]
        return total

    def norm_chunk(j):
        o, s = chunks[j]
        z_copy(j).wait_recv()

        def stats(n, carry):
            square, cross = carry
            cols = pl.ds(pl.multiple_of(n * tile_w, tile_w), tile_w)
            p = (
                part[4 * o:4 * o + s, cols].astype(f32)
                + sib_part[2 * o:2 * o + s, cols].astype(f32)
                + far_sum[o:o + s, cols].astype(f32)
            )
            proj[0:s, cols] = p
            scaled = ct[o:o + s, cols].astype(f32) * gain[:, cols]
            return square + fold(p * p), cross + fold(scaled * p)

        zero = jnp.zeros((s, 128), f32)
        square, cross = lax.fori_loop(0, n_w, stats, (zero, zero))
        inverse = lax.rsqrt(jnp.sum(square, axis=1, keepdims=True) / width + eps)
        slope = jnp.sum(cross, axis=1, keepdims=True) / width * inverse * inverse

        @pl.loop(0, n_w)
        def _(n):
            cols = pl.ds(pl.multiple_of(n * tile_w, tile_w), tile_w)
            scaled = ct[o:o + s, cols].astype(f32) * gain[:, cols]
            grad[4 * o:4 * o + s, cols] = (inverse * (scaled - proj[0:s, cols] * slope)).astype(bf16)

        grad_far(j).start()
        grad_core(j).start()

    lane = lax.broadcasted_iota(jnp.int32, (HEAD, 2 * side), 1)
    line = lax.broadcasted_iota(jnp.int32, (HEAD, 2 * side), 0)

    def pack_for(d, dst):
        to = lax.rem(xy + d, n_xy)
        head = jnp.full((HEAD, 2 * side), -1.0, f32)
        for h in range(planes):
            o = h * n_xy + to
            both = jnp.concatenate([coef[table[0, o]], coef[table[1, o]]], axis=1)
            dst[h * side:(h + 1) * side, :] = both.astype(bf16)
            place = jnp.where(lane < side, table[2, o].astype(f32), table[3, o].astype(f32))
            head = jnp.where(line == h, place, head)
        dst[planes * side:planes * side + HEAD, :] = head.astype(bf16)

    def pack_copy(d):
        return remote(
            pack.at[d], packs_in.at[d], pa_s.at[d], pa_r.at[d], xy_peer(d), tp
        )

    def pack_all():
        coef_load.wait()
        pack_for(0, packs_in.at[0])

        @pl.loop(1, n_xy)
        def _(d):
            pack_for(d, pack.at[d])
            pack_copy(d).start()

    half = lax.broadcasted_iota(jnp.int32, (1, 2 * side), 1)
    half = jnp.where(half < side, 0.0, 1.0).astype(f32)
    pairs = 4

    def sums_copy(e):
        return remote(
            sums_out.at[lax.rem(zh + e, planes)], sums_in.at[e], pb_s.at[e], pb_r.at[e],
            zh_peer(e), tp,
        )

    def sum_packs():
        @pl.loop(1, n_xy)
        def _(d):
            pack_copy(d).wait_recv()

        for h in range(planes):
            def add(d, totals):
                block = packs_in[d, h * side:(h + 1) * side, :].astype(f32)
                turned = pltpu.roll(block, side, 1)
                head = packs_in[d, planes * side:planes * side + HEAD, :].astype(f32)[h:h + 1, :]
                here = head - half
                there = pltpu.roll(jnp.broadcast_to(head, (8, 2 * side)), side, 1)[0:1, :] - half
                return tuple(
                    total
                    + jnp.where(here == 2.0 * p, block, 0.0)
                    + jnp.where(there == 2.0 * p, turned, 0.0)
                    for p, total in enumerate(totals)
                )

            zero = jnp.zeros((side, 2 * side), f32)
            totals = lax.fori_loop(0, n_xy, add, (zero,) * pairs)
            for p in range(pairs):
                sums[h, p * side:(p + 1) * side, :] = totals[p]
                sums_out[h, p * side:(p + 1) * side, :] = totals[p].astype(bf16)

        @pl.loop(1, planes)
        def _(e):
            sums_copy(e).start()

    def outer_step():
        @pl.loop(1, planes)
        def _(e):
            sums_copy(e).wait_recv()

        total = sums[zh]
        for e in range(1, planes):
            total = total + sums_in[e].astype(f32)
        for copy in (tiles_load, mom_load, left_load, right_load):
            copy.wait()
        wide = jnp.dot(total, right[...], precision=lax.Precision.HIGHEST)
        for p in range(pairs):
            decoded = jnp.dot(
                left[...], wide[p * side:(p + 1) * side, :], precision=lax.Precision.HIGHEST
            ) / n_rep
            for i in range(2):
                one = decoded[:, i * side:(i + 1) * side]
                fresh = momentum_decay * mom[2 * p + i] + one
                mom_new[2 * p + i] = fresh
                tiles_new[2 * p + i] = tiles[2 * p + i] - outer_rate * (one + momentum_decay * fresh)
        pltpu.make_async_copy(tiles_new, tiles_out, out_sem.at[0]).start()
        pltpu.make_async_copy(mom_new, mom_out, out_sem.at[1]).start()

    def ig_copies(j):
        o, s = chunks[j]
        out = []
        for p in range(PARTS):
            start = pl.multiple_of(order[p] * rows + o, 16)
            out.append(pltpu.make_async_copy(
                ig.at[pl.ds(4 * o + p * s, s)], ig_hbm.at[pl.ds(start, s)],
                ig_sem.at[j * PARTS + p],
            ))
        return out

    def input_chunk(j):
        o, s = chunks[j]
        ig[4 * o:4 * o + 4 * s, :] = lax.dot_general(
            grad[4 * o:4 * o + 4 * s, :], w[...], (((1,), (1,)), ((), ())),
            preferred_element_type=f32,
        ).astype(bf16)
        for copy in ig_copies(j):
            copy.start()

    def wg_copy(n):
        cols = pl.ds(pl.multiple_of(n * tile_w, tile_w), tile_w)
        return pltpu.make_async_copy(wg.at[:, cols], wg_hbm.at[:, cols], wg_sem.at[n])

    last = len(chunks) - 1
    early = 4 * chunks[last][0]

    for copy in loads:
        copy.wait()
    for j in range(last + 1):
        partial_chunk(j)
        if j == 0:
            pl.semaphore_wait(barrier, n_xy + planes)
        core_copy(j).start()
        if j == 0:
            pack_all()
        pair_chunk(j)
    attn_t[...] = attn[...].T
    ct_load.wait()
    gain_load.wait()
    norm_chunk(0)
    sum_packs()
    for j in range(1, last + 1):
        norm_chunk(j)
    outer_step()

    def arrived(j):
        grad_far(j).wait_recv()
        grad_forward(j).start()
        grad_core(j).wait_recv()

    for j in range(last):
        arrived(j)
        grad_forward(j).wait_recv()
        input_chunk(j)

    @pl.loop(0, n_w)
    def _(n):
        cols = pl.ds(pl.multiple_of(n * tile_w, tile_w), tile_w)
        acc[:, cols] = jnp.dot(
            attn_t[:, 0:early], grad[0:early, cols], preferred_element_type=f32
        )

    arrived(last)
    grad_forward(last).wait_recv()

    @pl.loop(0, n_w)
    def _(n):
        cols = pl.ds(pl.multiple_of(n * tile_w, tile_w), tile_w)
        wg[:, cols] = (
            acc[:, cols]
            + jnp.dot(attn_t[:, early:], grad[early:, cols], preferred_element_type=f32)
        ).astype(bf16)
        wg_copy(n).start()

    input_chunk(last)

    for j in range(last + 1):
        core_copy(j).wait_send()
        z_copy(j).wait_send()
        grad_far(j).wait_send()
        grad_core(j).wait_send()
        grad_forward(j).wait_send()
        for copy in ig_copies(j):
            copy.wait()

    @pl.loop(1, n_xy)
    def _(d):
        pack_copy(d).wait_send()

    @pl.loop(1, planes)
    def _(e):
        sums_copy(e).wait_send()

    pltpu.make_async_copy(tiles_new, tiles_out, out_sem.at[0]).wait()
    pltpu.make_async_copy(mom_new, mom_out, out_sem.at[1]).wait()

    @pl.loop(0, n_w)
    def _(n):
        wg_copy(n).wait()


def w_sem_width(width):
    return 512 if width % 512 == 0 else 256


def shards(attn_out, proj_weight, norm_gain, cotangent, coeffs, tile_ids, tiles, momentum):
    n_rep = lax.axis_size("rep")
    attended, weights, upstream = attn_out[0], proj_weight[0], cotangent[0]
    owned, side = tiles.shape[1], tiles.shape[2]
    tokens, depth = attended.shape
    width = weights.shape[1]
    rows = upstream.shape[0]
    n_w = width // w_sem_width(width)
    n_chunks = len(ROW_CHUNKS)
    n_xy = n_rep // PLANES
    kept = coeffs.shape[2]
    table = owner_table(tile_ids[0, 0], n_rep, owned)
    basis = dct_basis(side)
    right = np.zeros((2 * side, 2 * side), np.float32)
    right[:side, :side] = basis
    right[side:, side:] = basis
    f32, bf16 = jnp.float32, jnp.bfloat16
    dma = pltpu.SemaphoreType.DMA
    any_spec = pl.BlockSpec(memory_space=pl.ANY)
    message = PLANES * side + HEAD
    outs = pl.pallas_call(
        step_kernel,
        out_shape=(
            jax.ShapeDtypeStruct((depth, width), bf16),
            jax.ShapeDtypeStruct((tokens, depth), bf16),
            jax.ShapeDtypeStruct((owned, side, side), f32),
            jax.ShapeDtypeStruct((owned, side, side), f32),
        ),
        in_specs=[pl.BlockSpec(memory_space=pltpu.SMEM)] + [any_spec] * 9,
        out_specs=(any_spec,) * 4,
        scratch_shapes=[
            pltpu.VMEM((tokens, depth), bf16),
            pltpu.VMEM((depth, tokens), bf16),
            pltpu.VMEM((depth, width), bf16),
            pltpu.VMEM((1, width), f32),
            pltpu.VMEM((rows, width), bf16),
            pltpu.VMEM((kept, side, side), f32),
            pltpu.VMEM((owned, side, side), f32),
            pltpu.VMEM((owned, side, side), f32),
            pltpu.VMEM((side, side), f32),
            pltpu.VMEM((2 * side, 2 * side), f32),
            pltpu.VMEM((tokens, width), bf16),
            pltpu.VMEM((2 * rows, width), bf16),
            pltpu.VMEM((rows, width), bf16),
            pltpu.VMEM((rows, width), bf16),
            pltpu.VMEM((max(ROW_CHUNKS), width), f32),
            pltpu.VMEM((tokens, width), bf16),
            pltpu.VMEM((depth, width), f32),
            pltpu.VMEM((depth, width), bf16),
            pltpu.VMEM((tokens, depth), bf16),
            pltpu.VMEM((n_xy, message, 2 * side), bf16),
            pltpu.VMEM((n_xy, message, 2 * side), bf16),
            pltpu.VMEM((PLANES, owned // 2 * side, 2 * side), f32),
            pltpu.VMEM((PLANES, owned // 2 * side, 2 * side), bf16),
            pltpu.VMEM((PLANES, owned // 2 * side, 2 * side), bf16),
            pltpu.VMEM((owned, side, side), f32),
            pltpu.VMEM((owned, side, side), f32),
            dma((7,)), dma((n_w,)), dma((n_chunks * PARTS,)), dma((2,)), dma((n_w,)),
            dma((n_chunks * PARTS,)),
            *[dma((n_chunks,)) for _ in range(10)],
            dma((n_xy,)), dma((n_xy,)), dma((PLANES,)), dma((PLANES,)),
        ],
        compiler_params=pltpu.CompilerParams(
            collective_id=0, has_side_effects=True, vmem_limit_bytes=60 * 1024 * 1024
        ),
        cost_estimate=pl.CostEstimate(
            flops=6 * tokens * depth * width, bytes_accessed=16_000_000, transcendentals=0
        ),
    )(
        table, attended, weights, norm_gain, upstream, coeffs[0, 0], tiles[0], momentum[0],
        jnp.asarray(np.ascontiguousarray(basis.T)), jnp.asarray(right),
    )
    weight_grad, input_grad, tiles_new, momentum_new = outs
    return (weight_grad[None], input_grad[None], tiles_new[None], momentum_new[None])


def solution(mesh):
    in_specs = (
        P("rep", None, "tp"),
        P("rep", "tp", None),
        P("rep", None),
        P("rep", "tp", None),
        P("rep", "tp", None, None, None),
        P("rep", "tp", None),
        P("tp", "rep", None, None),
        P("tp", "rep", None, None),
    )
    out_specs = (
        P("rep", "tp", None),
        P("rep", None, "tp"),
        P("tp", "rep", None, None),
        P("tp", "rep", None, None),
    )
    return jax.shard_map(shards, mesh=mesh, in_specs=in_specs, out_specs=out_specs, check_vma=False)
```

```python
import jax
import jax.numpy as jnp
import numpy as np
from jax import lax
from jax.experimental import pallas as pl
from jax.experimental.pallas import tpu as pltpu
from jax.sharding import PartitionSpec as P

eps = 1e-06
outer_rate = 0.7
momentum_decay = 0.9
MESH = pl.DeviceIdType.MESH
PLANES = 4
PARTS = 4
HALVES = 2
FIRST = 4
STEP_VMEM = 55 * 1024 * 1024
WRITE_FROM = pl.ANY
HEAD = 16


def dct_basis(size):
    freq = np.arange(size, dtype=np.float64)[:, None]
    place = np.arange(size, dtype=np.float64)[None, :]
    scales = np.where(freq == 0, np.sqrt(1.0 / size), np.sqrt(2.0 / size))
    return (scales * np.cos(np.pi * (2.0 * place + 1.0) * freq / (2.0 * size))).astype(np.float32)


def owner_table(names, owners, owned):
    kept = names.shape[0]
    match = (names // owned)[None, :] == jnp.arange(owners, dtype=jnp.int32)[:, None]
    key = (jnp.arange(kept, dtype=jnp.int32) * owned + names % owned)[None, :]
    least = jnp.min(jnp.where(match, key, kept * owned - 1), axis=1)
    return jnp.stack([least, jnp.max(jnp.where(match, key, -1), axis=1)])


def step_kernel(
    table, attn_hbm, w_hbm, gain_hbm, ct_hbm, coef_hbm, tiles_hbm, mom_hbm, left_hbm, right_hbm,
    wg, ig, tiles_new, mom_new,
    attn, attn_t, w, gain, ct, coef, tiles, mom, left, right,
    part, sib_part, pair_sum, far_sum, proj, grad, acc, ig_acc,
    pack, packs_in, sums, near_out, near_in, last_out, last_in,
    in_sem, w_sem, attn_sem,
    core_s, core_r, z_s, z_r, gz_s, gz_r, gc_s, gc_r, gf_s, gf_r,
    pa_s, pa_r, pb_s, pb_r,
):
    n_rep = lax.axis_size("rep")
    planes = PLANES
    n_xy = n_rep // planes
    rep, tp = lax.axis_index("rep"), lax.axis_index("tp")
    xy, zh = lax.rem(rep, n_xy), lax.div(rep, n_xy)
    core, zl = lax.rem(tp, 2), lax.div(tp, 2)
    sib = zl * 2 + 1 - core
    far = (1 - zl) * 2 + core
    diag = (1 - zl) * 2 + 1 - core
    order = (tp, far, sib, diag)
    near = zh + 1 - 2 * lax.rem(zh, 2)
    next_near = planes - 1 - zh
    width = w.shape[1]
    rows = ct.shape[0]
    s = rows // HALVES
    tile_w = tile_width(width)
    n_w = width // tile_w
    side = coef.shape[1]
    owned = tiles.shape[0]
    pairs = owned // 2
    kept = coef.shape[0]
    f32, bf16 = jnp.float32, jnp.bfloat16

    def cols(n):
        return pl.ds(pl.multiple_of(n * tile_w, tile_w), tile_w)

    def xy_peer(d):
        return zh * n_xy + lax.rem(xy + d, n_xy)

    def plane_peer(z):
        return z * n_xy + xy

    loads = []
    for h in range(HALVES):
        for p in range(PARTS):
            start = pl.multiple_of(order[p] * rows + h * s, 16)
            loads.append(pltpu.make_async_copy(
                attn_hbm.at[pl.ds(start, s)],
                attn.at[pl.ds((h * PARTS + p) * s, s)],
                attn_sem.at[h * PARTS + p],
            ))
    for copy in loads:
        copy.start()

    def w_load(n):
        return pltpu.make_async_copy(w_hbm.at[:, cols(n)], w.at[:, cols(n)], w_sem.at[n])

    @pl.loop(0, n_w)
    def _(n):
        w_load(n).start()

    others = [
        pltpu.make_async_copy(src, dst, in_sem.at[i])
        for i, (src, dst) in enumerate(
            ((coef_hbm, coef), (ct_hbm, ct), (gain_hbm, gain), (tiles_hbm, tiles), (mom_hbm, mom),
             (left_hbm, left), (right_hbm, right))
        )
    ]
    coef_load, ct_load, gain_load, tiles_load, mom_load, left_load, right_load = others
    for copy in others:
        copy.start()

    barrier = pltpu.get_barrier_semaphore()
    for rep_to, tp_to in (
        (rep, sib), (rep, far), (plane_peer(near), tp), (plane_peer(next_near), tp)
    ):
        pl.semaphore_signal(barrier, inc=1, device_id=(rep_to, tp_to), device_id_type=MESH)

    @pl.loop(1, n_xy)
    def _(d):
        pl.semaphore_signal(barrier, inc=1, device_id=(xy_peer(d), tp), device_id_type=MESH)

    def remote(src, dst, send, recv, rep_to, tp_to):
        return pltpu.make_async_remote_copy(
            src_ref=src, dst_ref=dst, send_sem=send, recv_sem=recv,
            device_id=(rep_to, tp_to), device_id_type=MESH,
        )

    def core_copy(h, n):
        i = h * n_w + n
        return remote(
            part.at[pl.ds((h * PARTS + 2) * s, 2 * s), cols(n)],
            sib_part.at[pl.ds(h * 2 * s, 2 * s), cols(n)],
            core_s.at[i], core_r.at[i], rep, sib,
        )

    def z_copy(h, n):
        i = h * n_w + n
        here = pl.ds(h * s, s)
        return remote(
            pair_sum.at[here, cols(n)], far_sum.at[here, cols(n)], z_s.at[i], z_r.at[i], rep, far
        )

    def grad_copy(h, n, place, to, send, recv, target):
        i = h * n_w + n
        return remote(
            grad.at[pl.ds((h * PARTS + place) * s, s), cols(n)],
            grad.at[pl.ds((h * PARTS + to) * s, s), cols(n)],
            send.at[i], recv.at[i], rep, target,
        )

    def grad_far(h, n):
        return grad_copy(h, n, 0, 1, gz_s, gz_r, far)

    def grad_core(h, n):
        return grad_copy(h, n, 0, 2, gc_s, gc_r, sib)

    def grad_forward(h, n):
        return grad_copy(h, n, 1, 3, gf_s, gf_r, sib)

    def partial_tile(h, n):
        here = slice(h * PARTS * s, (h + 1) * PARTS * s)
        part[here, cols(n)] = jnp.dot(
            attn[here, :], w[:, cols(n)], preferred_element_type=f32
        ).astype(bf16)
        core_copy(h, n).start()

    def pair_tile(h, n):
        core_copy(h, n).wait_recv()
        base = h * PARTS * s + s
        pair_sum[h * s:h * s + s, cols(n)] = (
            part[base:base + s, cols(n)].astype(f32)
            + sib_part[h * 2 * s + s:(h + 1) * 2 * s, cols(n)].astype(f32)
        ).astype(bf16)
        z_copy(h, n).start()

    def fold(block):
        total = block[:, 0:128]
        for k in range(1, block.shape[1] // 128):
            total = total + block[:, k * 128:(k + 1) * 128]
        return total

    def norm_half(h):
        here = slice(h * s, h * s + s)
        base = h * PARTS * s

        def stats(n, carry):
            square, cross = carry
            z_copy(h, n).wait_recv()
            p = (
                part[base:base + s, cols(n)].astype(f32)
                + sib_part[h * 2 * s:h * 2 * s + s, cols(n)].astype(f32)
                + far_sum[here, cols(n)].astype(f32)
            )
            proj[:, cols(n)] = p
            scaled = ct[here, cols(n)].astype(f32) * gain[:, cols(n)]
            return square + fold(p * p), cross + fold(scaled * p)

        zero = jnp.zeros((s, 128), f32)
        square, cross = lax.fori_loop(0, n_w, stats, (zero, zero))
        inverse = lax.rsqrt(jnp.sum(square, axis=1, keepdims=True) / width + eps)
        slope = jnp.sum(cross, axis=1, keepdims=True) / width * inverse * inverse

        @pl.loop(0, n_w)
        def _(n):
            scaled = ct[here, cols(n)].astype(f32) * gain[:, cols(n)]
            grad[base:base + s, cols(n)] = (
                inverse * (scaled - proj[:, cols(n)] * slope)
            ).astype(bf16)
            grad_core(h, n).start()

    def send_far(h, low, high):
        @pl.loop(low, high)
        def _(n):
            grad_far(h, n).start()

    lane = lax.broadcasted_iota(jnp.int32, (HEAD, 2 * side), 1)
    line = lax.broadcasted_iota(jnp.int32, (HEAD, 2 * side), 0)

    def pack_for(d, dst):
        to = lax.rem(xy + d, n_xy)
        head = jnp.full((HEAD, 2 * side), -1.0, f32)
        for h in range(planes):
            o = h * n_xy + to
            least, most = table[0, o], table[1, o]
            one, two = least // owned, jnp.maximum(most, 0) // owned
            both = jnp.concatenate([coef[one], coef[two]], axis=1)
            dst[h * side:(h + 1) * side, :] = both.astype(bf16)
            one_place = jnp.where(most >= 0, least - one * owned, -1)
            two_place = jnp.where(most > least, most - two * owned, -1)
            place = jnp.where(lane < side, one_place.astype(f32), two_place.astype(f32))
            head = jnp.where(line == h, place, head)
        dst[planes * side:planes * side + HEAD, :] = head.astype(bf16)

    def pack_copy(d):
        return remote(pack.at[d], packs_in.at[d], pa_s.at[d], pa_r.at[d], xy_peer(d), tp)

    each = -(-n_xy // (n_w - 1))

    def pack_some(n):
        for i in range(each):
            d = (n - 1) * each + 1 + i

            @pl.when(d < n_xy)
            def _():
                pack_for(d, pack.at[d])
                pack_copy(d).start()

            @pl.when(d == n_xy)
            def _():
                pack_for(n_xy, packs_in.at[0])

    half = lax.broadcasted_iota(jnp.int32, (1, 2 * side), 1)
    half = jnp.where(half < side, 0.0, 1.0).astype(f32)

    def near_copy():
        return remote(near_out, near_in, pb_s.at[0], pb_r.at[0], plane_peer(near), tp)

    def last_copy():
        return remote(last_out, last_in, pb_s.at[1], pb_r.at[1], plane_peer(next_near), tp)

    def sum_packs():
        @pl.loop(1, n_xy)
        def _(d):
            pack_copy(d).wait_recv()

        for h in range(planes):
            def add(d, totals):
                block = packs_in[d, h * side:(h + 1) * side, :].astype(f32)
                turned = pltpu.roll(block, side, 1)
                head = packs_in[d, planes * side:planes * side + HEAD, :].astype(f32)[h:h + 1, :]
                here = head - half
                there = pltpu.roll(jnp.broadcast_to(head, (8, 2 * side)), side, 1)[0:1, :] - half
                return tuple(
                    total
                    + jnp.where(here == 2.0 * p, block, 0.0)
                    + jnp.where(there == 2.0 * p, turned, 0.0)
                    for p, total in enumerate(totals)
                )

            zero = jnp.zeros((side, 2 * side), f32)
            totals = lax.fori_loop(0, n_xy, add, (zero,) * pairs)
            for p in range(pairs):
                sums[h, p * side:(p + 1) * side, :] = totals[p]
        near_out[0] = sums[near].astype(bf16)
        near_out[1] = sums[planes - 1 - near].astype(bf16)
        near_copy().start()

    def pass_on():
        near_copy().wait_recv()
        last_out[...] = (sums[next_near] + near_in[1].astype(f32)).astype(bf16)
        last_copy().start()

    def outer_step():
        last_copy().wait_recv()
        total = sums[zh] + near_in[0].astype(f32) + last_in[...].astype(f32)
        for copy in (tiles_load, mom_load, left_load, right_load):
            copy.wait()
        wide = jnp.dot(total, right[...], precision=lax.Precision.HIGHEST)
        for p in range(pairs):
            decoded = jnp.dot(
                left[...], wide[p * side:(p + 1) * side, :], precision=lax.Precision.HIGHEST
            ) / n_rep
            for i in range(2):
                one = decoded[:, i * side:(i + 1) * side]
                fresh = momentum_decay * mom[2 * p + i] + one
                mom_new[2 * p + i] = fresh
                tiles_new[2 * p + i] = tiles[2 * p + i] - outer_rate * (one + momentum_decay * fresh)

    def arrive(h, n):
        grad_far(h, n).wait_recv()
        grad_forward(h, n).start()

    def use_tile(h, n):
        grad_core(h, n).wait_recv()
        grad_forward(h, n).wait_recv()
        here = slice(h * PARTS * s, (h + 1) * PARTS * s)
        block = grad[here, cols(n)]
        product = jnp.dot(attn_t[:, here], block, preferred_element_type=f32)
        if h == 0:
            acc[:, cols(n)] = product
        elif h < HALVES - 1:
            acc[:, cols(n)] += product
        else:
            wg[:, cols(n)] = (acc[:, cols(n)] + product).astype(bf16)
        ig_acc[here, :] += lax.dot_general(
            block, w[:, cols(n)], (((1,), (1,)), ((), ())), preferred_element_type=f32
        )

    def use_half(h, low, high):
        if low == 0:
            arrive(h, 0)

        @pl.loop(low, high)
        def _(n):
            @pl.when(n + 1 < n_w)
            def _():
                arrive(h, n + 1)

            use_tile(h, n)

    def finish_input(h):
        for p in range(PARTS):
            start = pl.multiple_of(order[p] * rows + h * s, 16)
            base = (h * PARTS + p) * s
            ig[pl.ds(start, s), :] = ig_acc[base:base + s, :].astype(bf16)

    for copy in loads:
        copy.wait()
    for h in range(HALVES):
        if h == 0:
            w_load(0).wait()
            pl.semaphore_wait(barrier, n_xy + 3)
        partial_tile(h, 0)

        @pl.loop(1, n_w)
        def _(n):
            if h == 0:
                w_load(n).wait()
            partial_tile(h, n)
            pair_tile(h, n - 1)
            if h == 0:
                @pl.when(n == 1)
                def _():
                    coef_load.wait()

                pack_some(n)

        pair_tile(h, n_w - 1)
    attn_t[...] = attn[...].T
    ig_acc[...] = jnp.zeros_like(ig_acc)
    ct_load.wait()
    gain_load.wait()
    first = min(FIRST, n_w - 1)
    norm_half(0)
    send_far(0, 0, first)
    sum_packs()
    send_far(0, first, n_w)
    norm_half(1)
    use_half(0, 0, first - 1)
    pass_on()
    send_far(1, 0, n_w)
    use_half(0, first - 1, n_w)
    finish_input(0)
    outer_step()
    use_half(1, 0, n_w)
    finish_input(1)

    for h in range(HALVES):
        @pl.loop(0, n_w)
        def _(n):
            core_copy(h, n).wait_send()
            z_copy(h, n).wait_send()
            grad_far(h, n).wait_send()
            grad_core(h, n).wait_send()
            grad_forward(h, n).wait_send()

    @pl.loop(1, n_xy)
    def _(d):
        pack_copy(d).wait_send()

    near_copy().wait_send()
    last_copy().wait_send()


def write_kernel(*refs):
    sources, targets, sem = refs[:4], refs[4:8], refs[8]
    pieces = 8
    step = sources[0].shape[0] // pieces
    copies = [
        pltpu.make_async_copy(
            sources[0].at[pl.ds(i * step, step)], targets[0].at[pl.ds(i * step, step)], sem.at[i]
        )
        for i in range(pieces)
    ]
    copies += [
        pltpu.make_async_copy(sources[i], targets[i], sem.at[pieces + i - 1]) for i in range(1, 4)
    ]
    for copy in copies:
        copy.start()
    for copy in copies:
        copy.wait()


def tile_width(width):
    return 512


def shards(attn_out, proj_weight, norm_gain, cotangent, coeffs, tile_ids, tiles, momentum):
    n_rep = lax.axis_size("rep")
    attended, weights, upstream = attn_out[0], proj_weight[0], cotangent[0]
    owned, side = tiles.shape[1], tiles.shape[2]
    tokens, depth = attended.shape
    width = weights.shape[1]
    rows = upstream.shape[0]
    n_w = width // tile_width(width)
    n_xy = n_rep // PLANES
    kept = coeffs.shape[2]
    table = owner_table(tile_ids[0, 0], n_rep, owned)
    basis = dct_basis(side)
    right = np.zeros((2 * side, 2 * side), np.float32)
    right[:side, :side] = basis
    right[side:, side:] = basis
    f32, bf16 = jnp.float32, jnp.bfloat16
    dma = pltpu.SemaphoreType.DMA
    any_spec = pl.BlockSpec(memory_space=pl.ANY)
    message = PLANES * side + HEAD
    summed = owned // 2 * side
    results = (
        ((depth, width), bf16),
        ((tokens, depth), bf16),
        ((owned, side, side), f32),
        ((owned, side, side), f32),
    )
    operands = (
        attended, weights, norm_gain, upstream, coeffs[0, 0], tiles[0], momentum[0],
        jnp.asarray(np.ascontiguousarray(basis.T)), jnp.asarray(right),
    )
    held = pl.pallas_call(
        step_kernel,
        out_shape=tuple(pltpu.VMEM(shape, dtype) for shape, dtype in results),
        in_specs=[pl.BlockSpec(memory_space=pltpu.SMEM)] + [any_spec] * len(operands),
        out_specs=(pl.BlockSpec(memory_space=pltpu.VMEM),) * 4,
        scratch_shapes=[
            pltpu.VMEM((tokens, depth), bf16),
            pltpu.VMEM((depth, tokens), bf16),
            pltpu.VMEM((depth, width), bf16),
            pltpu.VMEM((1, width), f32),
            pltpu.VMEM((rows, width), bf16),
            pltpu.VMEM((kept, side, side), f32),
            pltpu.VMEM((owned, side, side), f32),
            pltpu.VMEM((owned, side, side), f32),
            pltpu.VMEM((side, side), f32),
            pltpu.VMEM((2 * side, 2 * side), f32),
            pltpu.VMEM((tokens, width), bf16),
            pltpu.VMEM((2 * rows, width), bf16),
            pltpu.VMEM((rows, width), bf16),
            pltpu.VMEM((rows, width), bf16),
            pltpu.VMEM((rows // HALVES, width), f32),
            pltpu.VMEM((tokens, width), bf16),
            pltpu.VMEM((depth, width), f32),
            pltpu.VMEM((tokens, depth), f32),
            pltpu.VMEM((n_xy, message, 2 * side), bf16),
            pltpu.VMEM((n_xy, message, 2 * side), bf16),
            pltpu.VMEM((PLANES, summed, 2 * side), f32),
            pltpu.VMEM((2, summed, 2 * side), bf16),
            pltpu.VMEM((2, summed, 2 * side), bf16),
            pltpu.VMEM((summed, 2 * side), bf16),
            pltpu.VMEM((summed, 2 * side), bf16),
            dma((7,)), dma((n_w,)), dma((HALVES * PARTS,)),
            *[dma((HALVES * n_w,)) for _ in range(10)],
            dma((n_xy,)), dma((n_xy,)), dma((2,)), dma((2,)),
        ],
        compiler_params=pltpu.CompilerParams(
            collective_id=0, has_side_effects=True, vmem_limit_bytes=STEP_VMEM
        ),
        cost_estimate=pl.CostEstimate(
            flops=6 * tokens * depth * width, bytes_accessed=16_000_000, transcendentals=0
        ),
    )(table, *operands)
    outs = pl.pallas_call(
        write_kernel,
        out_shape=tuple(jax.ShapeDtypeStruct(shape, dtype) for shape, dtype in results),
        in_specs=[pl.BlockSpec(memory_space=WRITE_FROM)] * 4,
        out_specs=(any_spec,) * 4,
        scratch_shapes=[dma((11,))],
        compiler_params=pltpu.CompilerParams(vmem_limit_bytes=4 * 1024 * 1024),
    )(*held)
    return tuple(out[None] for out in outs)


def solution(mesh):
    in_specs = (
        P("rep", None, "tp"),
        P("rep", "tp", None),
        P("rep", None),
        P("rep", "tp", None),
        P("rep", "tp", None, None, None),
        P("rep", "tp", None),
        P("tp", "rep", None, None),
        P("tp", "rep", None, None),
    )
    out_specs = (
        P("rep", "tp", None),
        P("rep", None, "tp"),
        P("tp", "rep", None, None),
        P("tp", "rep", None, None),
    )
    return jax.shard_map(shards, mesh=mesh, in_specs=in_specs, out_specs=out_specs, check_vma=False)
```

```python
import jax
import jax.numpy as jnp
import numpy as np
from jax import lax
from jax.experimental import pallas as pl
from jax.experimental.pallas import tpu as pltpu
from jax.sharding import PartitionSpec as P

eps = 1e-06
outer_rate = 0.7
momentum_decay = 0.9
MESH = pl.DeviceIdType.MESH
PLANES = 4
PARTS = 4
HALVES = 2
WINDOW = 5
AHEAD = 3
STEP_VMEM = 55 * 1024 * 1024
WRITE_FROM = pl.ANY
HEAD = 16


def dct_basis(size):
    freq = np.arange(size, dtype=np.float64)[:, None]
    place = np.arange(size, dtype=np.float64)[None, :]
    scales = np.where(freq == 0, np.sqrt(1.0 / size), np.sqrt(2.0 / size))
    return (scales * np.cos(np.pi * (2.0 * place + 1.0) * freq / (2.0 * size))).astype(np.float32)


def step_kernel(
    ids_hbm, attn_hbm, w_hbm, gain_hbm, ct_hbm, coef_hbm, tiles_hbm, mom_hbm, left_hbm, right_hbm,
    wg, ig, tiles_new, mom_new,
    attn, attn_t, w, gain, ct, coef, tiles, mom, left, right,
    part, sib_part, pair_sum, far_sum, proj, grad, acc, ig_acc,
    pack, packs_in, sums, near_out, near_in, last_out, last_in,
    ids, keys, table,
    in_sem, w_sem, attn_sem,
    core_s, core_r, z_s, z_r, gz_s, gz_r, gc_s, gc_r, gf_s, gf_r,
    pa_s, pa_r, pb_s, pb_r,
):
    n_rep = lax.axis_size("rep")
    planes = PLANES
    n_xy = n_rep // planes
    rep, tp = lax.axis_index("rep"), lax.axis_index("tp")
    xy, zh = lax.rem(rep, n_xy), lax.div(rep, n_xy)
    core, zl = lax.rem(tp, 2), lax.div(tp, 2)
    sib = zl * 2 + 1 - core
    far = (1 - zl) * 2 + core
    diag = (1 - zl) * 2 + 1 - core
    order = (tp, far, sib, diag)
    near = zh + 1 - 2 * lax.rem(zh, 2)
    next_near = planes - 1 - zh
    width = w.shape[1]
    rows = ct.shape[0]
    s = rows // HALVES
    tile_w = tile_width(width)
    n_w = width // tile_w
    side = coef.shape[1]
    owned = tiles.shape[0]
    pairs = owned // 2
    kept = coef.shape[0]
    f32, bf16 = jnp.float32, jnp.bfloat16

    def cols(n):
        return pl.ds(pl.multiple_of(n * tile_w, tile_w), tile_w)

    def xy_peer(d):
        return zh * n_xy + lax.rem(xy + d, n_xy)

    def plane_peer(z):
        return z * n_xy + xy

    loads = []
    for h in range(HALVES):
        for p in range(PARTS):
            start = pl.multiple_of(order[p] * rows + h * s, 16)
            loads.append(pltpu.make_async_copy(
                attn_hbm.at[pl.ds(start, s)],
                attn.at[pl.ds((h * PARTS + p) * s, s)],
                attn_sem.at[h * PARTS + p],
            ))
    for copy in loads:
        copy.start()

    def w_load(n):
        return pltpu.make_async_copy(w_hbm.at[:, cols(n)], w.at[:, cols(n)], w_sem.at[n])

    for n in range(min(AHEAD, n_w)):
        w_load(n).start()

    others = [
        pltpu.make_async_copy(src, dst, in_sem.at[i])
        for i, (src, dst) in enumerate(
            ((ids_hbm, ids), (coef_hbm, coef), (ct_hbm, ct), (gain_hbm, gain), (tiles_hbm, tiles), (mom_hbm, mom),
             (left_hbm, left), (right_hbm, right))
        )
    ]
    ids_load, coef_load, ct_load, gain_load, tiles_load, mom_load, left_load, right_load = others
    ids_load.start()

    barrier = pltpu.get_barrier_semaphore()
    for rep_to, tp_to in (
        (rep, sib), (rep, far), (plane_peer(near), tp), (plane_peer(next_near), tp)
    ):
        pl.semaphore_signal(barrier, inc=1, device_id=(rep_to, tp_to), device_id_type=MESH)

    @pl.loop(1, n_xy)
    def _(d):
        pl.semaphore_signal(barrier, inc=1, device_id=(xy_peer(d), tp), device_id_type=MESH)

    def remote(src, dst, send, recv, rep_to, tp_to):
        return pltpu.make_async_remote_copy(
            src_ref=src, dst_ref=dst, send_sem=send, recv_sem=recv,
            device_id=(rep_to, tp_to), device_id_type=MESH,
        )

    def make_table():
        entry = lax.broadcasted_iota(jnp.int32, (n_rep, kept), 1)
        owner = lax.broadcasted_iota(jnp.int32, (n_rep, kept), 0)
        names = jnp.broadcast_to(ids[...], (n_rep, kept))
        match = (names >= owner * owned) & (names < owner * owned + owned)
        key = entry * owned + names - owner * owned
        least = jnp.min(jnp.where(match, key, kept * owned - 1), axis=1, keepdims=True)
        most = jnp.max(jnp.where(match, key, -1), axis=1, keepdims=True)
        lane = lax.broadcasted_iota(jnp.int32, keys.shape, 1)
        keys[...] = jnp.where(lane == 0, least, most)
        table_copy().start()

    def table_copy():
        return pltpu.make_async_copy(keys, table, in_sem.at[8])

    def core_copy(h, n):
        i = h * n_w + n
        return remote(
            part.at[pl.ds((h * PARTS + 2) * s, 2 * s), cols(n)],
            sib_part.at[pl.ds(h * 2 * s, 2 * s), cols(n)],
            core_s.at[i], core_r.at[i], rep, sib,
        )

    def z_copy(h, n):
        i = h * n_w + n
        here = pl.ds(h * s, s)
        return remote(
            pair_sum.at[here, cols(n)], far_sum.at[here, cols(n)], z_s.at[i], z_r.at[i], rep, far
        )

    def grad_copy(h, n, place, to, send, recv, target):
        i = h * n_w + n
        return remote(
            grad.at[pl.ds((h * PARTS + place) * s, s), cols(n)],
            grad.at[pl.ds((h * PARTS + to) * s, s), cols(n)],
            send.at[i], recv.at[i], rep, target,
        )

    def grad_far(h, n):
        return grad_copy(h, n, 0, 1, gz_s, gz_r, far)

    def grad_core(h, n):
        return grad_copy(h, n, 0, 2, gc_s, gc_r, sib)

    def grad_forward(h, n):
        return grad_copy(h, n, 1, 3, gf_s, gf_r, sib)

    def partial_tile(h, n):
        here = slice(h * PARTS * s, (h + 1) * PARTS * s)
        part[here, cols(n)] = jnp.dot(
            attn[here, :], w[:, cols(n)], preferred_element_type=f32
        ).astype(bf16)
        core_copy(h, n).start()

    def pair_tile(h, n):
        core_copy(h, n).wait_recv()
        behind(h, n, lambda a, b: z_copy(a, b).wait_send())
        base = h * PARTS * s + s
        pair_sum[h * s:h * s + s, cols(n)] = (
            part[base:base + s, cols(n)].astype(f32)
            + sib_part[h * 2 * s + s:(h + 1) * 2 * s, cols(n)].astype(f32)
        ).astype(bf16)
        z_copy(h, n).start()

    def behind(h, n, step):
        @pl.when(n >= window)
        def _():
            step(h, n - window)

        if h > 0:
            @pl.when(n < window)
            def _():
                step(h - 1, n + n_w - window)

    def ahead(h, n, step):
        @pl.when(n + window < n_w)
        def _():
            step(h, n + window)

        if h < HALVES - 1:
            @pl.when(n + window >= n_w)
            def _():
                step(h + 1, n + window - n_w)

    def fold(block):
        total = block[:, 0:128]
        for k in range(1, block.shape[1] // 128):
            total = total + block[:, k * 128:(k + 1) * 128]
        return total

    def norm_half(h):
        here = slice(h * s, h * s + s)
        base = h * PARTS * s

        def stats(n, carry):
            square, cross = carry
            z_copy(h, n).wait_recv()
            p = (
                part[base:base + s, cols(n)].astype(f32)
                + sib_part[h * 2 * s:h * 2 * s + s, cols(n)].astype(f32)
                + far_sum[here, cols(n)].astype(f32)
            )
            proj[:, cols(n)] = p
            scaled = ct[here, cols(n)].astype(f32) * gain[:, cols(n)]
            return square + fold(p * p), cross + fold(scaled * p)

        zero = jnp.zeros((s, 128), f32)
        square, cross = lax.fori_loop(0, n_w, stats, (zero, zero))
        inverse = lax.rsqrt(jnp.sum(square, axis=1, keepdims=True) / width + eps)
        slope = jnp.sum(cross, axis=1, keepdims=True) / width * inverse * inverse

        @pl.loop(0, n_w)
        def _(n):
            scaled = ct[here, cols(n)].astype(f32) * gain[:, cols(n)]
            grad[base:base + s, cols(n)] = (
                inverse * (scaled - proj[:, cols(n)] * slope)
            ).astype(bf16)
            grad_core(h, n).start()

    def send_far(h, low, high):
        @pl.loop(low, high)
        def _(n):
            grad_far(h, n).start()

    lane = lax.broadcasted_iota(jnp.int32, (HEAD, 2 * side), 1)
    line = lax.broadcasted_iota(jnp.int32, (HEAD, 2 * side), 0)

    def pack_for(d, dst):
        to = lax.rem(xy + d, n_xy)
        head = jnp.full((HEAD, 2 * side), -1.0, f32)
        for h in range(planes):
            o = h * n_xy + to
            least, most = table[o, 0], table[o, 1]
            one, two = least // owned, jnp.maximum(most, 0) // owned
            both = jnp.concatenate([coef[one], coef[two]], axis=1)
            dst[h * side:(h + 1) * side, :] = both.astype(bf16)
            one_place = jnp.where(most >= 0, least - one * owned, -1)
            two_place = jnp.where(most > least, most - two * owned, -1)
            place = jnp.where(lane < side, one_place.astype(f32), two_place.astype(f32))
            head = jnp.where(line == h, place, head)
        dst[planes * side:planes * side + HEAD, :] = head.astype(bf16)

    def pack_copy(d):
        return remote(pack.at[d], packs_in.at[d], pa_s.at[d], pa_r.at[d], xy_peer(d), tp)

    each = -(-n_xy // (n_w - 1))

    def pack_some(n):
        for i in range(each):
            d = (n - 1) * each + 1 + i

            @pl.when(d < n_xy)
            def _():
                pack_for(d, pack.at[d])
                pack_copy(d).start()

            @pl.when(d == n_xy)
            def _():
                pack_for(n_xy, packs_in.at[0])

    half = lax.broadcasted_iota(jnp.int32, (1, 2 * side), 1)
    half = jnp.where(half < side, 0.0, 1.0).astype(f32)

    def near_copy():
        return remote(near_out, near_in, pb_s.at[0], pb_r.at[0], plane_peer(near), tp)

    def last_copy():
        return remote(last_out, last_in, pb_s.at[1], pb_r.at[1], plane_peer(next_near), tp)

    def sum_packs():
        @pl.loop(1, n_xy)
        def _(d):
            pack_copy(d).wait_recv()

        for h in range(planes):
            def add(d, totals):
                block = packs_in[d, h * side:(h + 1) * side, :].astype(f32)
                turned = pltpu.roll(block, side, 1)
                head = packs_in[d, planes * side:planes * side + HEAD, :].astype(f32)[h:h + 1, :]
                here = head - half
                there = pltpu.roll(jnp.broadcast_to(head, (8, 2 * side)), side, 1)[0:1, :] - half
                return tuple(
                    total
                    + jnp.where(here == 2.0 * p, block, 0.0)
                    + jnp.where(there == 2.0 * p, turned, 0.0)
                    for p, total in enumerate(totals)
                )

            zero = jnp.zeros((side, 2 * side), f32)
            totals = lax.fori_loop(0, n_xy, add, (zero,) * pairs)
            for p in range(pairs):
                sums[h, p * side:(p + 1) * side, :] = totals[p]
        near_out[0] = sums[near].astype(bf16)
        near_out[1] = sums[planes - 1 - near].astype(bf16)
        near_copy().start()

    def pass_on():
        near_copy().wait_recv()
        last_out[...] = (sums[next_near] + near_in[1].astype(f32)).astype(bf16)
        last_copy().start()

    def outer_step():
        last_copy().wait_recv()
        total = sums[zh] + near_in[0].astype(f32) + last_in[...].astype(f32)
        for copy in (tiles_load, mom_load, left_load, right_load):
            copy.wait()
        wide = jnp.dot(total, right[...], precision=lax.Precision.HIGHEST)
        for p in range(pairs):
            decoded = jnp.dot(
                left[...], wide[p * side:(p + 1) * side, :], precision=lax.Precision.HIGHEST
            ) / n_rep
            for i in range(2):
                one = decoded[:, i * side:(i + 1) * side]
                fresh = momentum_decay * mom[2 * p + i] + one
                mom_new[2 * p + i] = fresh
                tiles_new[2 * p + i] = tiles[2 * p + i] - outer_rate * (one + momentum_decay * fresh)

    def arrive(h, n):
        grad_far(h, n).wait_recv()
        grad_forward(h, n).start()
        grad_far(h, n).wait_send()
        ahead(h, n, lambda a, b: grad_far(a, b).start())

    def use_tile(h, n):
        grad_core(h, n).wait_recv()
        grad_forward(h, n).wait_recv()
        here = slice(h * PARTS * s, (h + 1) * PARTS * s)
        block = grad[here, cols(n)]
        product = jnp.dot(attn_t[:, here], block, preferred_element_type=f32)
        if h == 0:
            acc[:, cols(n)] = product
        elif h < HALVES - 1:
            acc[:, cols(n)] += product
        else:
            wg[:, cols(n)] = (acc[:, cols(n)] + product).astype(bf16)
        ig_acc[here, :] += lax.dot_general(
            block, w[:, cols(n)], (((1,), (1,)), ((), ())), preferred_element_type=f32
        )

    def use_half(h, low, high):
        if low == 0:
            arrive(h, 0)

        @pl.loop(low, high)
        def _(n):
            @pl.when(n + 1 < n_w)
            def _():
                arrive(h, n + 1)

            use_tile(h, n)

    def finish_input(h):
        for p in range(PARTS):
            start = pl.multiple_of(order[p] * rows + h * s, 16)
            base = (h * PARTS + p) * s
            ig[pl.ds(start, s), :] = ig_acc[base:base + s, :].astype(bf16)

    window = min(WINDOW, n_w)
    for h in range(HALVES):
        for copy in loads[h * PARTS:(h + 1) * PARTS]:
            copy.wait()
        if h == 0:
            w_load(0).wait()
            pl.semaphore_wait(barrier, n_xy + 3)
        partial_tile(h, 0)
        if h == 0:
            for copy in others[1:]:
                copy.start()
            ids_load.wait()
            make_table()

        @pl.loop(1, n_w)
        def _(n):
            if h == 0:
                @pl.when(n + AHEAD - 1 < n_w)
                def _():
                    w_load(n + AHEAD - 1).start()

                w_load(n).wait()
            partial_tile(h, n)
            pair_tile(h, n - 1)
            if h == 0:
                @pl.when(n == 1)
                def _():
                    table_copy().wait()
                    coef_load.wait()

                pack_some(n)

        pair_tile(h, n_w - 1)
    attn_t[...] = attn[...].T
    ig_acc[...] = jnp.zeros_like(ig_acc)
    ct_load.wait()
    gain_load.wait()
    norm_half(0)
    send_far(0, 0, window)
    sum_packs()
    norm_half(1)
    use_half(0, 0, window)
    pass_on()
    use_half(0, window, n_w)
    finish_input(0)
    outer_step()
    use_half(1, 0, n_w)
    finish_input(1)

    for h in range(HALVES):
        @pl.loop(0, n_w)
        def _(n):
            core_copy(h, n).wait_send()
            grad_core(h, n).wait_send()
            grad_forward(h, n).wait_send()

    @pl.loop(n_w - window, n_w)
    def _(n):
        z_copy(HALVES - 1, n).wait_send()

    @pl.loop(1, n_xy)
    def _(d):
        pack_copy(d).wait_send()

    near_copy().wait_send()
    last_copy().wait_send()


def write_kernel(*refs):
    sources, targets, sem = refs[:4], refs[4:8], refs[8]
    pieces = 8
    step = sources[0].shape[0] // pieces
    copies = [
        pltpu.make_async_copy(
            sources[0].at[pl.ds(i * step, step)], targets[0].at[pl.ds(i * step, step)], sem.at[i]
        )
        for i in range(pieces)
    ]
    copies += [
        pltpu.make_async_copy(sources[i], targets[i], sem.at[pieces + i - 1]) for i in range(1, 4)
    ]
    for copy in copies:
        copy.start()
    for copy in copies:
        copy.wait()


def tile_width(width):
    return 512


def shards(attn_out, proj_weight, norm_gain, cotangent, coeffs, tile_ids, tiles, momentum):
    n_rep = lax.axis_size("rep")
    attended, weights, upstream = attn_out[0], proj_weight[0], cotangent[0]
    owned, side = tiles.shape[1], tiles.shape[2]
    tokens, depth = attended.shape
    width = weights.shape[1]
    rows = upstream.shape[0]
    n_w = width // tile_width(width)
    n_xy = n_rep // PLANES
    kept = coeffs.shape[2]
    basis = dct_basis(side)
    right = np.zeros((2 * side, 2 * side), np.float32)
    right[:side, :side] = basis
    right[side:, side:] = basis
    f32, bf16 = jnp.float32, jnp.bfloat16
    dma = pltpu.SemaphoreType.DMA
    any_spec = pl.BlockSpec(memory_space=pl.ANY)
    message = PLANES * side + HEAD
    summed = owned // 2 * side
    results = (
        ((depth, width), bf16),
        ((tokens, depth), bf16),
        ((owned, side, side), f32),
        ((owned, side, side), f32),
    )
    operands = (
        tile_ids[0], attended, weights, norm_gain, upstream, coeffs[0, 0], tiles[0], momentum[0],
        jnp.asarray(np.ascontiguousarray(basis.T)), jnp.asarray(right),
    )
    held = pl.pallas_call(
        step_kernel,
        out_shape=tuple(pltpu.VMEM(shape, dtype) for shape, dtype in results),
        in_specs=[any_spec] * len(operands),
        out_specs=(pl.BlockSpec(memory_space=pltpu.VMEM),) * 4,
        scratch_shapes=[
            pltpu.VMEM((tokens, depth), bf16),
            pltpu.VMEM((depth, tokens), bf16),
            pltpu.VMEM((depth, width), bf16),
            pltpu.VMEM((1, width), f32),
            pltpu.VMEM((rows, width), bf16),
            pltpu.VMEM((kept, side, side), f32),
            pltpu.VMEM((owned, side, side), f32),
            pltpu.VMEM((owned, side, side), f32),
            pltpu.VMEM((side, side), f32),
            pltpu.VMEM((2 * side, 2 * side), f32),
            pltpu.VMEM((tokens, width), bf16),
            pltpu.VMEM((2 * rows, width), bf16),
            pltpu.VMEM((rows, width), bf16),
            pltpu.VMEM((rows, width), bf16),
            pltpu.VMEM((rows // HALVES, width), f32),
            pltpu.VMEM((tokens, width), bf16),
            pltpu.VMEM((depth, width), f32),
            pltpu.VMEM((tokens, depth), f32),
            pltpu.VMEM((n_xy, message, 2 * side), bf16),
            pltpu.VMEM((n_xy, message, 2 * side), bf16),
            pltpu.VMEM((PLANES, summed, 2 * side), f32),
            pltpu.VMEM((2, summed, 2 * side), bf16),
            pltpu.VMEM((2, summed, 2 * side), bf16),
            pltpu.VMEM((summed, 2 * side), bf16),
            pltpu.VMEM((summed, 2 * side), bf16),
            pltpu.VMEM((1, kept), jnp.int32),
            pltpu.VMEM((n_rep, 128), jnp.int32),
            pltpu.SMEM((n_rep, 128), jnp.int32),
            dma((9,)), dma((n_w,)), dma((HALVES * PARTS,)),
            *[dma((HALVES * n_w,)) for _ in range(10)],
            dma((n_xy,)), dma((n_xy,)), dma((2,)), dma((2,)),
        ],
        compiler_params=pltpu.CompilerParams(
            collective_id=0, has_side_effects=True, vmem_limit_bytes=STEP_VMEM
        ),
        cost_estimate=pl.CostEstimate(
            flops=6 * tokens * depth * width, bytes_accessed=16_000_000, transcendentals=0
        ),
    )(*operands)
    outs = pl.pallas_call(
        write_kernel,
        out_shape=tuple(jax.ShapeDtypeStruct(shape, dtype) for shape, dtype in results),
        in_specs=[pl.BlockSpec(memory_space=WRITE_FROM)] * 4,
        out_specs=(any_spec,) * 4,
        scratch_shapes=[dma((11,))],
        compiler_params=pltpu.CompilerParams(vmem_limit_bytes=4 * 1024 * 1024),
    )(*held)
    return tuple(out[None] for out in outs)


def solution(mesh):
    in_specs = (
        P("rep", None, "tp"),
        P("rep", "tp", None),
        P("rep", None),
        P("rep", "tp", None),
        P("rep", "tp", None, None, None),
        P("rep", "tp", None),
        P("tp", "rep", None, None),
        P("tp", "rep", None, None),
    )
    out_specs = (
        P("rep", "tp", None),
        P("rep", None, "tp"),
        P("tp", "rep", None, None),
        P("tp", "rep", None, None),
    )
    return jax.shard_map(shards, mesh=mesh, in_specs=in_specs, out_specs=out_specs, check_vma=False)
```

```python
import jax
import jax.numpy as jnp
import numpy as np
from jax import lax
from jax.experimental import pallas as pl
from jax.experimental.pallas import tpu as pltpu
from jax.sharding import PartitionSpec as P

eps = 1e-06
outer_rate = 0.7
momentum_decay = 0.9
MESH = pl.DeviceIdType.MESH
PLANES = 4
PARTS = 4
HALVES = 2
WINDOW = 5
AHEAD = 3
STEP_VMEM = 55 * 1024 * 1024
WRITE_FROM = pl.ANY
HEAD = 16


def dct_basis(size):
    freq = np.arange(size, dtype=np.float64)[:, None]
    place = np.arange(size, dtype=np.float64)[None, :]
    scales = np.where(freq == 0, np.sqrt(1.0 / size), np.sqrt(2.0 / size))
    return (scales * np.cos(np.pi * (2.0 * place + 1.0) * freq / (2.0 * size))).astype(np.float32)


def step_kernel(
    ids_hbm, attn_hbm, w_hbm, gain_hbm, ct_hbm, coef_hbm, tiles_hbm, mom_hbm, left_hbm, right_hbm,
    wg, ig, tiles_new, mom_new,
    attn, attn_t, w, gain, ct, coef, tiles, mom, left, right,
    part, sib_part, pair_sum, far_sum, proj, grad, acc, ig_acc,
    pack, packs_in, sums, near_out, near_in, last_out, last_in,
    ids, keys, table,
    in_sem, w_sem, attn_sem,
    core_s, core_r, z_s, z_r, gz_s, gz_r, gc_s, gc_r, gf_s, gf_r,
    pa_s, pa_r, pb_s, pb_r, ready, go,
):
    n_rep = lax.axis_size("rep")
    planes = PLANES
    n_xy = n_rep // planes
    rep, tp = lax.axis_index("rep"), lax.axis_index("tp")
    xy, zh = lax.rem(rep, n_xy), lax.div(rep, n_xy)
    core, zl = lax.rem(tp, 2), lax.div(tp, 2)
    sib = zl * 2 + 1 - core
    far = (1 - zl) * 2 + core
    diag = (1 - zl) * 2 + 1 - core
    order = (tp, far, sib, diag)
    near = zh + 1 - 2 * lax.rem(zh, 2)
    next_near = planes - 1 - zh
    width = w.shape[1]
    rows = ct.shape[0]
    s = rows // HALVES
    tile_w = tile_width(width)
    n_w = width // tile_w
    side = coef.shape[1]
    owned = tiles.shape[0]
    pairs = owned // 2
    kept = coef.shape[0]
    f32, bf16 = jnp.float32, jnp.bfloat16

    def cols(n):
        return pl.ds(pl.multiple_of(n * tile_w, tile_w), tile_w)

    def xy_peer(d):
        return zh * n_xy + lax.rem(xy + d, n_xy)

    def plane_peer(z):
        return z * n_xy + xy

    loads = []
    for h in range(HALVES):
        for p in range(PARTS):
            start = pl.multiple_of(order[p] * rows + h * s, 16)
            loads.append(pltpu.make_async_copy(
                attn_hbm.at[pl.ds(start, s)],
                attn.at[pl.ds((h * PARTS + p) * s, s)],
                attn_sem.at[h * PARTS + p],
            ))
    for copy in loads:
        copy.start()

    def w_load(n):
        return pltpu.make_async_copy(w_hbm.at[:, cols(n)], w.at[:, cols(n)], w_sem.at[n])

    for n in range(min(AHEAD, n_w)):
        w_load(n).start()

    others = [
        pltpu.make_async_copy(src, dst, in_sem.at[i])
        for i, (src, dst) in enumerate(
            ((ids_hbm, ids), (coef_hbm, coef), (ct_hbm, ct), (gain_hbm, gain), (tiles_hbm, tiles), (mom_hbm, mom),
             (left_hbm, left), (right_hbm, right))
        )
    ]
    ids_load, coef_load, ct_load, gain_load, tiles_load, mom_load, left_load, right_load = others
    ids_load.start()

    barrier = pltpu.get_barrier_semaphore()
    middle = (tp == 1) | (tp == 2)

    @pl.when(jnp.logical_not(middle))
    def _():
        for to in (sib, far):
            pl.semaphore_signal(barrier, inc=1, device_id=(rep, to), device_id_type=MESH)

    @pl.when(middle)
    def _():
        pl.semaphore_wait(barrier, 2)
        for to in (sib, far):
            pl.semaphore_signal(ready, inc=1, device_id=(rep, to), device_id_type=MESH)

    def greet_replicas():
        @pl.when(jnp.logical_not(middle))
        def _():
            pl.semaphore_wait(ready, 2)

        @pl.when(tp == 0)
        def _():
            for z in (near, next_near):
                pl.semaphore_signal(
                    barrier, inc=1, device_id=(plane_peer(z), 0), device_id_type=MESH
                )

            @pl.loop(1, n_xy)
            def _(d):
                pl.semaphore_signal(barrier, inc=1, device_id=(xy_peer(d), 0), device_id_type=MESH)

    def meet_replicas():
        @pl.when(tp == 0)
        def _():
            pl.semaphore_wait(barrier, n_xy + 1)
            for to in range(1, PARTS):
                pl.semaphore_signal(go, inc=1, device_id=(rep, to), device_id_type=MESH)

        @pl.when(tp != 0)
        def _():
            pl.semaphore_wait(go, 1)

    def remote(src, dst, send, recv, rep_to, tp_to):
        return pltpu.make_async_remote_copy(
            src_ref=src, dst_ref=dst, send_sem=send, recv_sem=recv,
            device_id=(rep_to, tp_to), device_id_type=MESH,
        )

    def make_table():
        entry = lax.broadcasted_iota(jnp.int32, (n_rep, kept), 1)
        owner = lax.broadcasted_iota(jnp.int32, (n_rep, kept), 0)
        names = jnp.broadcast_to(ids[...], (n_rep, kept))
        match = (names >= owner * owned) & (names < owner * owned + owned)
        key = entry * owned + names - owner * owned
        least = jnp.min(jnp.where(match, key, kept * owned - 1), axis=1, keepdims=True)
        most = jnp.max(jnp.where(match, key, -1), axis=1, keepdims=True)
        lane = lax.broadcasted_iota(jnp.int32, keys.shape, 1)
        keys[...] = jnp.where(lane == 0, least, most)
        table_copy().start()

    def table_copy():
        return pltpu.make_async_copy(keys, table, in_sem.at[8])

    def core_copy(h, n):
        i = h * n_w + n
        return remote(
            part.at[pl.ds((h * PARTS + 2) * s, 2 * s), cols(n)],
            sib_part.at[pl.ds(h * 2 * s, 2 * s), cols(n)],
            core_s.at[i], core_r.at[i], rep, sib,
        )

    def z_copy(h, n):
        i = h * n_w + n
        here = pl.ds(h * s, s)
        return remote(
            pair_sum.at[here, cols(n)], far_sum.at[here, cols(n)], z_s.at[i], z_r.at[i], rep, far
        )

    def grad_copy(h, n, place, to, send, recv, target):
        i = h * n_w + n
        return remote(
            grad.at[pl.ds((h * PARTS + place) * s, s), cols(n)],
            grad.at[pl.ds((h * PARTS + to) * s, s), cols(n)],
            send.at[i], recv.at[i], rep, target,
        )

    def grad_far(h, n):
        return grad_copy(h, n, 0, 1, gz_s, gz_r, far)

    def grad_core(h, n):
        return grad_copy(h, n, 0, 2, gc_s, gc_r, sib)

    def grad_forward(h, n):
        return grad_copy(h, n, 1, 3, gf_s, gf_r, sib)

    def partial_tile(h, n):
        here = slice(h * PARTS * s, (h + 1) * PARTS * s)
        part[here, cols(n)] = jnp.dot(
            attn[here, :], w[:, cols(n)], preferred_element_type=f32
        ).astype(bf16)
        core_copy(h, n).start()

    def pair_tile(h, n):
        core_copy(h, n).wait_recv()
        behind(h, n, lambda a, b: z_copy(a, b).wait_send())
        base = h * PARTS * s + s
        pair_sum[h * s:h * s + s, cols(n)] = (
            part[base:base + s, cols(n)].astype(f32)
            + sib_part[h * 2 * s + s:(h + 1) * 2 * s, cols(n)].astype(f32)
        ).astype(bf16)
        z_copy(h, n).start()

    def behind(h, n, step):
        @pl.when(n >= window)
        def _():
            step(h, n - window)

        if h > 0:
            @pl.when(n < window)
            def _():
                step(h - 1, n + n_w - window)

    def ahead(h, n, step):
        @pl.when(n + window < n_w)
        def _():
            step(h, n + window)

        if h < HALVES - 1:
            @pl.when(n + window >= n_w)
            def _():
                step(h + 1, n + window - n_w)

    def fold(block):
        total = block[:, 0:128]
        for k in range(1, block.shape[1] // 128):
            total = total + block[:, k * 128:(k + 1) * 128]
        return total

    def norm_half(h):
        here = slice(h * s, h * s + s)
        base = h * PARTS * s

        def stats(n, carry):
            square, cross = carry
            z_copy(h, n).wait_recv()
            p = (
                part[base:base + s, cols(n)].astype(f32)
                + sib_part[h * 2 * s:h * 2 * s + s, cols(n)].astype(f32)
                + far_sum[here, cols(n)].astype(f32)
            )
            proj[:, cols(n)] = p
            scaled = ct[here, cols(n)].astype(f32) * gain[:, cols(n)]
            return square + fold(p * p), cross + fold(scaled * p)

        zero = jnp.zeros((s, 128), f32)
        square, cross = lax.fori_loop(0, n_w, stats, (zero, zero))
        inverse = lax.rsqrt(jnp.sum(square, axis=1, keepdims=True) / width + eps)
        slope = jnp.sum(cross, axis=1, keepdims=True) / width * inverse * inverse

        @pl.loop(0, n_w)
        def _(n):
            scaled = ct[here, cols(n)].astype(f32) * gain[:, cols(n)]
            grad[base:base + s, cols(n)] = (
                inverse * (scaled - proj[:, cols(n)] * slope)
            ).astype(bf16)
            grad_core(h, n).start()

    def send_far(h, low, high):
        @pl.loop(low, high)
        def _(n):
            grad_far(h, n).start()

    lane = lax.broadcasted_iota(jnp.int32, (HEAD, 2 * side), 1)
    line = lax.broadcasted_iota(jnp.int32, (HEAD, 2 * side), 0)

    def pack_for(d, dst):
        to = lax.rem(xy + d, n_xy)
        head = jnp.full((HEAD, 2 * side), -1.0, f32)
        for h in range(planes):
            o = h * n_xy + to
            least, most = table[o, 0], table[o, 1]
            one, two = least // owned, jnp.maximum(most, 0) // owned
            both = jnp.concatenate([coef[one], coef[two]], axis=1)
            dst[h * side:(h + 1) * side, :] = both.astype(bf16)
            one_place = jnp.where(most >= 0, least - one * owned, -1)
            two_place = jnp.where(most > least, most - two * owned, -1)
            place = jnp.where(lane < side, one_place.astype(f32), two_place.astype(f32))
            head = jnp.where(line == h, place, head)
        dst[planes * side:planes * side + HEAD, :] = head.astype(bf16)

    def pack_copy(d):
        return remote(pack.at[d], packs_in.at[d], pa_s.at[d], pa_r.at[d], xy_peer(d), tp)

    each = -(-n_xy // (n_w - 1))

    def pack_some(n):
        for i in range(each):
            d = (n - 1) * each + 1 + i

            @pl.when(d < n_xy)
            def _():
                pack_for(d, pack.at[d])
                pack_copy(d).start()

            @pl.when(d == n_xy)
            def _():
                pack_for(n_xy, packs_in.at[0])

    half = lax.broadcasted_iota(jnp.int32, (1, 2 * side), 1)
    half = jnp.where(half < side, 0.0, 1.0).astype(f32)

    def near_copy():
        return remote(near_out, near_in, pb_s.at[0], pb_r.at[0], plane_peer(near), tp)

    def last_copy():
        return remote(last_out, last_in, pb_s.at[1], pb_r.at[1], plane_peer(next_near), tp)

    def sum_packs():
        @pl.loop(1, n_xy)
        def _(d):
            pack_copy(d).wait_recv()

        for h in range(planes):
            def add(d, totals):
                block = packs_in[d, h * side:(h + 1) * side, :].astype(f32)
                turned = pltpu.roll(block, side, 1)
                head = packs_in[d, planes * side:planes * side + HEAD, :].astype(f32)[h:h + 1, :]
                here = head - half
                there = pltpu.roll(jnp.broadcast_to(head, (8, 2 * side)), side, 1)[0:1, :] - half
                return tuple(
                    total
                    + jnp.where(here == 2.0 * p, block, 0.0)
                    + jnp.where(there == 2.0 * p, turned, 0.0)
                    for p, total in enumerate(totals)
                )

            zero = jnp.zeros((side, 2 * side), f32)
            totals = lax.fori_loop(0, n_xy, add, (zero,) * pairs)
            for p in range(pairs):
                sums[h, p * side:(p + 1) * side, :] = totals[p]
        near_out[0] = sums[near].astype(bf16)
        near_out[1] = sums[planes - 1 - near].astype(bf16)
        near_copy().start()

    def pass_on():
        near_copy().wait_recv()
        last_out[...] = (sums[next_near] + near_in[1].astype(f32)).astype(bf16)
        last_copy().start()

    def outer_step():
        last_copy().wait_recv()
        total = sums[zh] + near_in[0].astype(f32) + last_in[...].astype(f32)
        for copy in (tiles_load, mom_load, left_load, right_load):
            copy.wait()
        wide = jnp.dot(total, right[...], precision=lax.Precision.HIGHEST)
        for p in range(pairs):
            decoded = jnp.dot(
                left[...], wide[p * side:(p + 1) * side, :], precision=lax.Precision.HIGHEST
            ) / n_rep
            for i in range(2):
                one = decoded[:, i * side:(i + 1) * side]
                fresh = momentum_decay * mom[2 * p + i] + one
                mom_new[2 * p + i] = fresh
                tiles_new[2 * p + i] = tiles[2 * p + i] - outer_rate * (one + momentum_decay * fresh)

    def arrive(h, n):
        grad_far(h, n).wait_recv()
        grad_forward(h, n).start()
        grad_far(h, n).wait_send()
        ahead(h, n, lambda a, b: grad_far(a, b).start())

    def use_tile(h, n):
        grad_core(h, n).wait_recv()
        grad_forward(h, n).wait_recv()
        here = slice(h * PARTS * s, (h + 1) * PARTS * s)
        block = grad[here, cols(n)]
        product = jnp.dot(attn_t[:, here], block, preferred_element_type=f32)
        if h == 0:
            acc[:, cols(n)] = product
        elif h < HALVES - 1:
            acc[:, cols(n)] += product
        else:
            wg[:, cols(n)] = (acc[:, cols(n)] + product).astype(bf16)
        ig_acc[here, :] += lax.dot_general(
            block, w[:, cols(n)], (((1,), (1,)), ((), ())), preferred_element_type=f32
        )

    def use_half(h, low, high):
        if low == 0:
            arrive(h, 0)

        @pl.loop(low, high)
        def _(n):
            @pl.when(n + 1 < n_w)
            def _():
                arrive(h, n + 1)

            use_tile(h, n)

    def finish_input(h):
        for p in range(PARTS):
            start = pl.multiple_of(order[p] * rows + h * s, 16)
            base = (h * PARTS + p) * s
            ig[pl.ds(start, s), :] = ig_acc[base:base + s, :].astype(bf16)

    window = min(WINDOW, n_w)
    for h in range(HALVES):
        for copy in loads[h * PARTS:(h + 1) * PARTS]:
            copy.wait()
        if h == 0:
            w_load(0).wait()
            greet_replicas()
        partial_tile(h, 0)
        if h == 0:
            for copy in others[1:]:
                copy.start()
            ids_load.wait()
            make_table()

        @pl.loop(1, n_w)
        def _(n):
            if h == 0:
                @pl.when(n + AHEAD - 1 < n_w)
                def _():
                    w_load(n + AHEAD - 1).start()

                w_load(n).wait()
            partial_tile(h, n)
            pair_tile(h, n - 1)
            if h == HALVES - 1:
                @pl.when(n == 1)
                def _():
                    meet_replicas()
                    table_copy().wait()
                    coef_load.wait()

                pack_some(n)

        pair_tile(h, n_w - 1)
    attn_t[...] = attn[...].T
    ig_acc[...] = jnp.zeros_like(ig_acc)
    ct_load.wait()
    gain_load.wait()
    norm_half(0)
    send_far(0, 0, window)
    norm_half(1)
    use_half(0, 0, n_w - 4)
    sum_packs()
    use_half(0, n_w - 4, n_w)
    finish_input(0)
    pass_on()
    use_half(1, 0, n_w - 3)
    outer_step()
    use_half(1, n_w - 3, n_w)
    finish_input(1)

    for h in range(HALVES):
        @pl.loop(0, n_w)
        def _(n):
            core_copy(h, n).wait_send()
            grad_core(h, n).wait_send()
            grad_forward(h, n).wait_send()

    @pl.loop(n_w - window, n_w)
    def _(n):
        z_copy(HALVES - 1, n).wait_send()

    @pl.loop(1, n_xy)
    def _(d):
        pack_copy(d).wait_send()

    near_copy().wait_send()
    last_copy().wait_send()


def write_kernel(*refs):
    sources, targets, sem = refs[:4], refs[4:8], refs[8]
    pieces = 8
    step = sources[0].shape[0] // pieces
    copies = [
        pltpu.make_async_copy(
            sources[0].at[pl.ds(i * step, step)], targets[0].at[pl.ds(i * step, step)], sem.at[i]
        )
        for i in range(pieces)
    ]
    copies += [
        pltpu.make_async_copy(sources[i], targets[i], sem.at[pieces + i - 1]) for i in range(1, 4)
    ]
    for copy in copies:
        copy.start()
    for copy in copies:
        copy.wait()


def tile_width(width):
    return 512


def shards(attn_out, proj_weight, norm_gain, cotangent, coeffs, tile_ids, tiles, momentum):
    n_rep = lax.axis_size("rep")
    attended, weights, upstream = attn_out[0], proj_weight[0], cotangent[0]
    owned, side = tiles.shape[1], tiles.shape[2]
    tokens, depth = attended.shape
    width = weights.shape[1]
    rows = upstream.shape[0]
    n_w = width // tile_width(width)
    n_xy = n_rep // PLANES
    kept = coeffs.shape[2]
    basis = dct_basis(side)
    right = np.zeros((2 * side, 2 * side), np.float32)
    right[:side, :side] = basis
    right[side:, side:] = basis
    f32, bf16 = jnp.float32, jnp.bfloat16
    dma = pltpu.SemaphoreType.DMA
    any_spec = pl.BlockSpec(memory_space=pl.ANY)
    message = PLANES * side + HEAD
    summed = owned // 2 * side
    results = (
        ((depth, width), bf16),
        ((tokens, depth), bf16),
        ((owned, side, side), f32),
        ((owned, side, side), f32),
    )
    operands = (
        tile_ids[0], attended, weights, norm_gain, upstream, coeffs[0, 0], tiles[0], momentum[0],
        jnp.asarray(np.ascontiguousarray(basis.T)), jnp.asarray(right),
    )
    held = pl.pallas_call(
        step_kernel,
        out_shape=tuple(pltpu.VMEM(shape, dtype) for shape, dtype in results),
        in_specs=[any_spec] * len(operands),
        out_specs=(pl.BlockSpec(memory_space=pltpu.VMEM),) * 4,
        scratch_shapes=[
            pltpu.VMEM((tokens, depth), bf16),
            pltpu.VMEM((depth, tokens), bf16),
            pltpu.VMEM((depth, width), bf16),
            pltpu.VMEM((1, width), f32),
            pltpu.VMEM((rows, width), bf16),
            pltpu.VMEM((kept, side, side), f32),
            pltpu.VMEM((owned, side, side), f32),
            pltpu.VMEM((owned, side, side), f32),
            pltpu.VMEM((side, side), f32),
            pltpu.VMEM((2 * side, 2 * side), f32),
            pltpu.VMEM((tokens, width), bf16),
            pltpu.VMEM((2 * rows, width), bf16),
            pltpu.VMEM((rows, width), bf16),
            pltpu.VMEM((rows, width), bf16),
            pltpu.VMEM((rows // HALVES, width), f32),
            pltpu.VMEM((tokens, width), bf16),
            pltpu.VMEM((depth, width), f32),
            pltpu.VMEM((tokens, depth), f32),
            pltpu.VMEM((n_xy, message, 2 * side), bf16),
            pltpu.VMEM((n_xy, message, 2 * side), bf16),
            pltpu.VMEM((PLANES, summed, 2 * side), f32),
            pltpu.VMEM((2, summed, 2 * side), bf16),
            pltpu.VMEM((2, summed, 2 * side), bf16),
            pltpu.VMEM((summed, 2 * side), bf16),
            pltpu.VMEM((summed, 2 * side), bf16),
            pltpu.VMEM((1, kept), jnp.int32),
            pltpu.VMEM((n_rep, 128), jnp.int32),
            pltpu.SMEM((n_rep, 128), jnp.int32),
            dma((9,)), dma((n_w,)), dma((HALVES * PARTS,)),
            *[dma((HALVES * n_w,)) for _ in range(10)],
            dma((n_xy,)), dma((n_xy,)), dma((2,)), dma((2,)),
            pltpu.SemaphoreType.REGULAR, pltpu.SemaphoreType.REGULAR,
        ],
        compiler_params=pltpu.CompilerParams(
            collective_id=0, has_side_effects=True, vmem_limit_bytes=STEP_VMEM
        ),
        cost_estimate=pl.CostEstimate(
            flops=6 * tokens * depth * width, bytes_accessed=16_000_000, transcendentals=0
        ),
    )(*operands)
    outs = pl.pallas_call(
        write_kernel,
        out_shape=tuple(jax.ShapeDtypeStruct(shape, dtype) for shape, dtype in results),
        in_specs=[pl.BlockSpec(memory_space=WRITE_FROM)] * 4,
        out_specs=(any_spec,) * 4,
        scratch_shapes=[dma((11,))],
        compiler_params=pltpu.CompilerParams(vmem_limit_bytes=4 * 1024 * 1024),
    )(*held)
    return tuple(out[None] for out in outs)


def solution(mesh):
    in_specs = (
        P("rep", None, "tp"),
        P("rep", "tp", None),
        P("rep", None),
        P("rep", "tp", None),
        P("rep", "tp", None, None, None),
        P("rep", "tp", None),
        P("tp", "rep", None, None),
        P("tp", "rep", None, None),
    )
    out_specs = (
        P("rep", "tp", None),
        P("rep", None, "tp"),
        P("tp", "rep", None, None),
        P("tp", "rep", None, None),
    )
    return jax.shard_map(shards, mesh=mesh, in_specs=in_specs, out_specs=out_specs, check_vma=False)
```

```python
import jax
import jax.numpy as jnp
import numpy as np
from jax import lax
from jax.experimental import pallas as pl
from jax.experimental.pallas import tpu as pltpu
from jax.sharding import PartitionSpec as P

eps = 1e-06
outer_rate = 0.7
momentum_decay = 0.9
MESH = pl.DeviceIdType.MESH
PLANES = 4
PARTS = 4
HALVES = 2
WINDOW = 5
EARLY = 3
AHEAD = 3
STEP_VMEM = 55 * 1024 * 1024
WRITE_FROM = pl.ANY
HEAD = 16


def dct_basis(size):
    freq = np.arange(size, dtype=np.float64)[:, None]
    place = np.arange(size, dtype=np.float64)[None, :]
    scales = np.where(freq == 0, np.sqrt(1.0 / size), np.sqrt(2.0 / size))
    return (scales * np.cos(np.pi * (2.0 * place + 1.0) * freq / (2.0 * size))).astype(np.float32)


def step_kernel(
    ids_hbm, attn_hbm, w_hbm, gain_hbm, ct_hbm, coef_hbm, tiles_hbm, mom_hbm, left_hbm, right_hbm,
    wg, ig, tiles_new, mom_new,
    attn, attn_t, w, gain, ct, coef, tiles, mom, left, right,
    part, sib_part, pair_sum, far_sum, proj, grad, acc, ig_acc,
    pack, packs_in, sums, near_out, near_in, last_out, last_in,
    ids, keys, table,
    in_sem, w_sem, attn_sem,
    core_s, core_r, z_s, z_r, gz_s, gz_r, gc_s, gc_r, gf_s, gf_r,
    pa_s, pa_r, pb_s, pb_r, ready, go,
):
    n_rep = lax.axis_size("rep")
    planes = PLANES
    n_xy = n_rep // planes
    rep, tp = lax.axis_index("rep"), lax.axis_index("tp")
    xy, zh = lax.rem(rep, n_xy), lax.div(rep, n_xy)
    core, zl = lax.rem(tp, 2), lax.div(tp, 2)
    sib = zl * 2 + 1 - core
    far = (1 - zl) * 2 + core
    diag = (1 - zl) * 2 + 1 - core
    order = (tp, far, sib, diag)
    near = zh + 1 - 2 * lax.rem(zh, 2)
    next_near = planes - 1 - zh
    width = w.shape[1]
    rows = ct.shape[0]
    s = rows // HALVES
    tile_w = tile_width(width)
    n_w = width // tile_w
    side = coef.shape[1]
    owned = tiles.shape[0]
    pairs = owned // 2
    kept = coef.shape[0]
    f32, bf16 = jnp.float32, jnp.bfloat16

    def cols(n):
        return pl.ds(pl.multiple_of(n * tile_w, tile_w), tile_w)

    def xy_peer(d):
        return zh * n_xy + lax.rem(xy + d, n_xy)

    def plane_peer(z):
        return z * n_xy + xy

    loads = []
    for h in range(HALVES):
        for p in range(PARTS):
            start = pl.multiple_of(order[p] * rows + h * s, 16)
            loads.append(pltpu.make_async_copy(
                attn_hbm.at[pl.ds(start, s)],
                attn.at[pl.ds((h * PARTS + p) * s, s)],
                attn_sem.at[h * PARTS + p],
            ))
    for copy in loads:
        copy.start()

    def w_load(n):
        return pltpu.make_async_copy(w_hbm.at[:, cols(n)], w.at[:, cols(n)], w_sem.at[n])

    for n in range(min(AHEAD, n_w)):
        w_load(n).start()

    others = [
        pltpu.make_async_copy(src, dst, in_sem.at[i])
        for i, (src, dst) in enumerate(
            ((ids_hbm, ids), (coef_hbm, coef), (ct_hbm, ct), (gain_hbm, gain), (tiles_hbm, tiles), (mom_hbm, mom),
             (left_hbm, left), (right_hbm, right))
        )
    ]
    ids_load, coef_load, ct_load, gain_load, tiles_load, mom_load, left_load, right_load = others
    ids_load.start()

    barrier = pltpu.get_barrier_semaphore()
    middle = (tp == 1) | (tp == 2)

    @pl.when(jnp.logical_not(middle))
    def _():
        for to in (sib, far):
            pl.semaphore_signal(barrier, inc=1, device_id=(rep, to), device_id_type=MESH)

    @pl.when(middle)
    def _():
        pl.semaphore_wait(barrier, 2)
        for to in (sib, far):
            pl.semaphore_signal(ready, inc=1, device_id=(rep, to), device_id_type=MESH)

    def greet_replicas():
        @pl.when(jnp.logical_not(middle))
        def _():
            pl.semaphore_wait(ready, 2)

        @pl.when(tp == 0)
        def _():
            for z in (near, next_near):
                pl.semaphore_signal(
                    barrier, inc=1, device_id=(plane_peer(z), 0), device_id_type=MESH
                )

            @pl.loop(1, n_xy)
            def _(d):
                pl.semaphore_signal(barrier, inc=1, device_id=(xy_peer(d), 0), device_id_type=MESH)

    def meet_replicas():
        @pl.when(tp == 0)
        def _():
            pl.semaphore_wait(barrier, n_xy + 1)
            for to in range(1, PARTS):
                pl.semaphore_signal(go, inc=1, device_id=(rep, to), device_id_type=MESH)

        @pl.when(tp != 0)
        def _():
            pl.semaphore_wait(go, 1)

    def remote(src, dst, send, recv, rep_to, tp_to):
        return pltpu.make_async_remote_copy(
            src_ref=src, dst_ref=dst, send_sem=send, recv_sem=recv,
            device_id=(rep_to, tp_to), device_id_type=MESH,
        )

    def make_table():
        entry = lax.broadcasted_iota(jnp.int32, (n_rep, kept), 1)
        owner = lax.broadcasted_iota(jnp.int32, (n_rep, kept), 0)
        names = jnp.broadcast_to(ids[...], (n_rep, kept))
        match = (names >= owner * owned) & (names < owner * owned + owned)
        key = entry * owned + names - owner * owned
        least = jnp.min(jnp.where(match, key, kept * owned - 1), axis=1, keepdims=True)
        most = jnp.max(jnp.where(match, key, -1), axis=1, keepdims=True)
        lane = lax.broadcasted_iota(jnp.int32, keys.shape, 1)
        keys[...] = jnp.where(lane == 0, least, most)
        table_copy().start()

    def table_copy():
        return pltpu.make_async_copy(keys, table, in_sem.at[8])

    def core_copy(h, n):
        i = h * n_w + n
        return remote(
            part.at[pl.ds((h * PARTS + 2) * s, 2 * s), cols(n)],
            sib_part.at[pl.ds(h * 2 * s, 2 * s), cols(n)],
            core_s.at[i], core_r.at[i], rep, sib,
        )

    def z_copy(h, n):
        i = h * n_w + n
        here = pl.ds(h * s, s)
        return remote(
            pair_sum.at[here, cols(n)], far_sum.at[here, cols(n)], z_s.at[i], z_r.at[i], rep, far
        )

    def grad_copy(h, n, place, to, send, recv, target):
        i = h * n_w + n
        return remote(
            grad.at[pl.ds((h * PARTS + place) * s, s), cols(n)],
            grad.at[pl.ds((h * PARTS + to) * s, s), cols(n)],
            send.at[i], recv.at[i], rep, target,
        )

    def grad_far(h, n):
        return grad_copy(h, n, 0, 1, gz_s, gz_r, far)

    def grad_core(h, n):
        return grad_copy(h, n, 0, 2, gc_s, gc_r, sib)

    def grad_forward(h, n):
        return grad_copy(h, n, 1, 3, gf_s, gf_r, sib)

    def partial_tile(h, n):
        here = slice(h * PARTS * s, (h + 1) * PARTS * s)
        part[here, cols(n)] = jnp.dot(
            attn[here, :], w[:, cols(n)], preferred_element_type=f32
        ).astype(bf16)

    def pair_tile(h, n):
        core_copy(h, n).wait_recv()
        behind(h, n, lambda a, b: z_copy(a, b).wait_send())
        base = h * PARTS * s + s
        pair_sum[h * s:h * s + s, cols(n)] = (
            part[base:base + s, cols(n)].astype(f32)
            + sib_part[h * 2 * s + s:(h + 1) * 2 * s, cols(n)].astype(f32)
        ).astype(bf16)
        z_copy(h, n).start()

    def behind(h, n, step):
        @pl.when(n >= window)
        def _():
            step(h, n - window)

        if h > 0:
            @pl.when(n < window)
            def _():
                step(h - 1, n + n_w - window)

    def ahead(h, n, step):
        @pl.when(n + window < n_w)
        def _():
            step(h, n + window)

        if h < HALVES - 1:
            @pl.when(n + window >= n_w)
            def _():
                step(h + 1, n + window - n_w)

    def fold(block):
        total = block[:, 0:128]
        for k in range(1, block.shape[1] // 128):
            total = total + block[:, k * 128:(k + 1) * 128]
        return total

    def norm_half(h):
        here = slice(h * s, h * s + s)
        base = h * PARTS * s

        def stats(n, carry):
            square, cross = carry
            z_copy(h, n).wait_recv()
            p = (
                part[base:base + s, cols(n)].astype(f32)
                + sib_part[h * 2 * s:h * 2 * s + s, cols(n)].astype(f32)
                + far_sum[here, cols(n)].astype(f32)
            )
            proj[:, cols(n)] = p
            scaled = ct[here, cols(n)].astype(f32) * gain[:, cols(n)]
            return square + fold(p * p), cross + fold(scaled * p)

        zero = jnp.zeros((s, 128), f32)
        square, cross = lax.fori_loop(0, n_w, stats, (zero, zero))
        inverse = lax.rsqrt(jnp.sum(square, axis=1, keepdims=True) / width + eps)
        slope = jnp.sum(cross, axis=1, keepdims=True) / width * inverse * inverse

        @pl.loop(0, n_w)
        def _(n):
            scaled = ct[here, cols(n)].astype(f32) * gain[:, cols(n)]
            grad[base:base + s, cols(n)] = (
                inverse * (scaled - proj[:, cols(n)] * slope)
            ).astype(bf16)
            grad_core(h, n).start()

    def send_far(h, low, high):
        @pl.loop(low, high)
        def _(n):
            grad_far(h, n).start()

    lane = lax.broadcasted_iota(jnp.int32, (HEAD, 2 * side), 1)
    line = lax.broadcasted_iota(jnp.int32, (HEAD, 2 * side), 0)

    def pack_for(d, dst):
        to = lax.rem(xy + d, n_xy)
        head = jnp.full((HEAD, 2 * side), -1.0, f32)
        for h in range(planes):
            o = h * n_xy + to
            least, most = table[o, 0], table[o, 1]
            one, two = least // owned, jnp.maximum(most, 0) // owned
            both = jnp.concatenate([coef[one], coef[two]], axis=1)
            dst[h * side:(h + 1) * side, :] = both.astype(bf16)
            one_place = jnp.where(most >= 0, least - one * owned, -1)
            two_place = jnp.where(most > least, most - two * owned, -1)
            place = jnp.where(lane < side, one_place.astype(f32), two_place.astype(f32))
            head = jnp.where(line == h, place, head)
        dst[planes * side:planes * side + HEAD, :] = head.astype(bf16)

    def pack_copy(d):
        return remote(pack.at[d], packs_in.at[d], pa_s.at[d], pa_r.at[d], xy_peer(d), tp)

    each = -(-n_xy // (n_w - 1))

    def pack_some(n):
        for i in range(each):
            d = (n - 1) * each + 1 + i

            @pl.when(d < n_xy)
            def _():
                pack_for(d, pack.at[d])
                pack_copy(d).start()

            @pl.when(d == n_xy)
            def _():
                pack_for(n_xy, packs_in.at[0])

    half = lax.broadcasted_iota(jnp.int32, (1, 2 * side), 1)
    half = jnp.where(half < side, 0.0, 1.0).astype(f32)

    def near_copies(slot):
        return [
            remote(
                near_out.at[slot, pl.ds(p * side, side)], near_in.at[slot, pl.ds(p * side, side)],
                pb_s.at[slot * pairs + p], pb_r.at[slot * pairs + p], plane_peer(near), tp,
            )
            for p in range(pairs)
        ]

    def last_copies():
        return [
            remote(
                last_out.at[pl.ds(p * side, side)], last_in.at[pl.ds(p * side, side)],
                pb_s.at[2 * pairs + p], pb_r.at[2 * pairs + p], plane_peer(next_near), tp,
            )
            for p in range(pairs)
        ]

    def sum_plane(z):
        here_rows = pl.ds(pl.multiple_of(z * side, side), side)

        def add(d, totals):
            block = packs_in[d, here_rows, :].astype(f32)
            turned = pltpu.roll(block, side, 1)
            head = packs_in[d, planes * side:planes * side + HEAD, :].astype(f32)
            head = jnp.sum(jnp.where(line == z, head, 0.0), axis=0, keepdims=True)
            here = head - half
            there = pltpu.roll(jnp.broadcast_to(head, (8, 2 * side)), side, 1)[0:1, :] - half
            return tuple(
                total
                + jnp.where(here == 2.0 * p, block, 0.0)
                + jnp.where(there == 2.0 * p, turned, 0.0)
                for p, total in enumerate(totals)
            )

        zero = jnp.zeros((side, 2 * side), f32)
        return lax.fori_loop(0, n_xy, add, (zero,) * pairs)

    def sum_packs():
        @pl.loop(1, n_xy)
        def _(d):
            pack_copy(d).wait_recv()

        for slot, z in ((1, planes - 1 - near), (0, near)):
            for p, total in enumerate(sum_plane(z)):
                near_out[slot, p * side:(p + 1) * side, :] = total.astype(bf16)
            for copy in near_copies(slot):
                copy.start()
        for slot, z in ((1, next_near), (0, zh)):
            for p, total in enumerate(sum_plane(z)):
                sums[slot, p * side:(p + 1) * side, :] = total

    def pass_on():
        for copy in near_copies(1):
            copy.wait_recv()
        last_out[...] = (sums[1] + near_in[1].astype(f32)).astype(bf16)
        for copy in last_copies():
            copy.start()

    def outer_step():
        for copy in near_copies(0) + last_copies():
            copy.wait_recv()
        total = sums[0] + near_in[0].astype(f32) + last_in[...].astype(f32)
        for copy in (tiles_load, mom_load, left_load, right_load):
            copy.wait()
        wide = jnp.dot(total, right[...], precision=lax.Precision.HIGHEST)
        for p in range(pairs):
            decoded = jnp.dot(
                left[...], wide[p * side:(p + 1) * side, :], precision=lax.Precision.HIGHEST
            ) / n_rep
            for i in range(2):
                one = decoded[:, i * side:(i + 1) * side]
                fresh = momentum_decay * mom[2 * p + i] + one
                mom_new[2 * p + i] = fresh
                tiles_new[2 * p + i] = tiles[2 * p + i] - outer_rate * (one + momentum_decay * fresh)

    def arrive(h, n):
        grad_far(h, n).wait_recv()
        grad_forward(h, n).start()
        grad_far(h, n).wait_send()
        ahead(h, n, lambda a, b: grad_far(a, b).start())

    def use_tile(h, n):
        grad_core(h, n).wait_recv()
        grad_forward(h, n).wait_recv()
        here = slice(h * PARTS * s, (h + 1) * PARTS * s)
        block = grad[here, cols(n)]
        product = jnp.dot(attn_t[:, here], block, preferred_element_type=f32)
        if h == 0:
            acc[:, cols(n)] = product
        elif h < HALVES - 1:
            acc[:, cols(n)] += product
        else:
            wg[:, cols(n)] = (acc[:, cols(n)] + product).astype(bf16)
        ig_acc[here, :] += lax.dot_general(
            block, w[:, cols(n)], (((1,), (1,)), ((), ())), preferred_element_type=f32
        )

    def use_half(h, low, high):
        if low == 0:
            arrive(h, 0)

        @pl.loop(low, high)
        def _(n):
            @pl.when(n + 1 < n_w)
            def _():
                arrive(h, n + 1)

            use_tile(h, n)

    def finish_input(h):
        for p in range(PARTS):
            start = pl.multiple_of(order[p] * rows + h * s, 16)
            base = (h * PARTS + p) * s
            ig[pl.ds(start, s), :] = ig_acc[base:base + s, :].astype(bf16)

    window = min(WINDOW, n_w)
    for h in range(HALVES):
        for copy in loads[h * PARTS:(h + 1) * PARTS]:
            copy.wait()
        if h == 0:
            w_load(0).wait()
        partial_tile(h, 0)
        if h == 0:
            greet_replicas()
        core_copy(h, 0).start()
        if h == 0:
            for copy in others[1:]:
                copy.start()
            ids_load.wait()
            make_table()

        @pl.loop(1, n_w)
        def _(n):
            if h == 0:
                @pl.when(n + AHEAD - 1 < n_w)
                def _():
                    w_load(n + AHEAD - 1).start()

                w_load(n).wait()
            partial_tile(h, n)
            core_copy(h, n).start()
            pair_tile(h, n - 1)
            if h == HALVES - 1:
                @pl.when(n == 1)
                def _():
                    meet_replicas()
                    table_copy().wait()
                    coef_load.wait()

                pack_some(n)

        pair_tile(h, n_w - 1)
    attn_t[...] = attn[...].T
    ig_acc[...] = jnp.zeros_like(ig_acc)
    ct_load.wait()
    gain_load.wait()
    norm_half(0)
    send_far(0, 0, window)
    norm_half(1)
    use_half(0, 0, EARLY)
    sum_packs()
    use_half(0, EARLY, n_w)
    finish_input(0)
    pass_on()
    use_half(1, 0, n_w - 3)
    outer_step()
    use_half(1, n_w - 3, n_w)
    finish_input(1)

    for h in range(HALVES):
        @pl.loop(0, n_w)
        def _(n):
            core_copy(h, n).wait_send()
            grad_core(h, n).wait_send()
            grad_forward(h, n).wait_send()

    @pl.loop(n_w - window, n_w)
    def _(n):
        z_copy(HALVES - 1, n).wait_send()

    @pl.loop(1, n_xy)
    def _(d):
        pack_copy(d).wait_send()

    for copy in near_copies(0) + near_copies(1) + last_copies():
        copy.wait_send()


def write_kernel(*refs):
    sources, targets, sem = refs[:4], refs[4:8], refs[8]
    pieces = 8
    step = sources[0].shape[0] // pieces
    copies = [
        pltpu.make_async_copy(
            sources[0].at[pl.ds(i * step, step)], targets[0].at[pl.ds(i * step, step)], sem.at[i]
        )
        for i in range(pieces)
    ]
    copies += [
        pltpu.make_async_copy(sources[i], targets[i], sem.at[pieces + i - 1]) for i in range(1, 4)
    ]
    for copy in copies:
        copy.start()
    for copy in copies:
        copy.wait()


def tile_width(width):
    return 512


def shards(attn_out, proj_weight, norm_gain, cotangent, coeffs, tile_ids, tiles, momentum):
    n_rep = lax.axis_size("rep")
    attended, weights, upstream = attn_out[0], proj_weight[0], cotangent[0]
    owned, side = tiles.shape[1], tiles.shape[2]
    tokens, depth = attended.shape
    width = weights.shape[1]
    rows = upstream.shape[0]
    n_w = width // tile_width(width)
    n_xy = n_rep // PLANES
    kept = coeffs.shape[2]
    basis = dct_basis(side)
    right = np.zeros((2 * side, 2 * side), np.float32)
    right[:side, :side] = basis
    right[side:, side:] = basis
    f32, bf16 = jnp.float32, jnp.bfloat16
    dma = pltpu.SemaphoreType.DMA
    any_spec = pl.BlockSpec(memory_space=pl.ANY)
    message = PLANES * side + HEAD
    summed = owned // 2 * side
    results = (
        ((depth, width), bf16),
        ((tokens, depth), bf16),
        ((owned, side, side), f32),
        ((owned, side, side), f32),
    )
    operands = (
        tile_ids[0], attended, weights, norm_gain, upstream, coeffs[0, 0], tiles[0], momentum[0],
        jnp.asarray(np.ascontiguousarray(basis.T)), jnp.asarray(right),
    )
    held = pl.pallas_call(
        step_kernel,
        out_shape=tuple(pltpu.VMEM(shape, dtype) for shape, dtype in results),
        in_specs=[any_spec] * len(operands),
        out_specs=(pl.BlockSpec(memory_space=pltpu.VMEM),) * 4,
        scratch_shapes=[
            pltpu.VMEM((tokens, depth), bf16),
            pltpu.VMEM((depth, tokens), bf16),
            pltpu.VMEM((depth, width), bf16),
            pltpu.VMEM((1, width), f32),
            pltpu.VMEM((rows, width), bf16),
            pltpu.VMEM((kept, side, side), f32),
            pltpu.VMEM((owned, side, side), f32),
            pltpu.VMEM((owned, side, side), f32),
            pltpu.VMEM((side, side), f32),
            pltpu.VMEM((2 * side, 2 * side), f32),
            pltpu.VMEM((tokens, width), bf16),
            pltpu.VMEM((2 * rows, width), bf16),
            pltpu.VMEM((rows, width), bf16),
            pltpu.VMEM((rows, width), bf16),
            pltpu.VMEM((rows // HALVES, width), f32),
            pltpu.VMEM((tokens, width), bf16),
            pltpu.VMEM((depth, width), f32),
            pltpu.VMEM((tokens, depth), f32),
            pltpu.VMEM((n_xy, message, 2 * side), bf16),
            pltpu.VMEM((n_xy, message, 2 * side), bf16),
            pltpu.VMEM((2, summed, 2 * side), f32),
            pltpu.VMEM((2, summed, 2 * side), bf16),
            pltpu.VMEM((2, summed, 2 * side), bf16),
            pltpu.VMEM((summed, 2 * side), bf16),
            pltpu.VMEM((summed, 2 * side), bf16),
            pltpu.VMEM((1, kept), jnp.int32),
            pltpu.VMEM((n_rep, 128), jnp.int32),
            pltpu.SMEM((n_rep, 128), jnp.int32),
            dma((9,)), dma((n_w,)), dma((HALVES * PARTS,)),
            *[dma((HALVES * n_w,)) for _ in range(10)],
            dma((n_xy,)), dma((n_xy,)), dma((3 * (owned // 2),)), dma((3 * (owned // 2),)),
            pltpu.SemaphoreType.REGULAR, pltpu.SemaphoreType.REGULAR,
        ],
        compiler_params=pltpu.CompilerParams(
            collective_id=0, has_side_effects=True, vmem_limit_bytes=STEP_VMEM
        ),
        cost_estimate=pl.CostEstimate(
            flops=6 * tokens * depth * width, bytes_accessed=16_000_000, transcendentals=0
        ),
    )(*operands)
    outs = pl.pallas_call(
        write_kernel,
        out_shape=tuple(jax.ShapeDtypeStruct(shape, dtype) for shape, dtype in results),
        in_specs=[pl.BlockSpec(memory_space=WRITE_FROM)] * 4,
        out_specs=(any_spec,) * 4,
        scratch_shapes=[dma((11,))],
        compiler_params=pltpu.CompilerParams(vmem_limit_bytes=4 * 1024 * 1024),
    )(*held)
    return tuple(out[None] for out in outs)


def solution(mesh):
    in_specs = (
        P("rep", None, "tp"),
        P("rep", "tp", None),
        P("rep", None),
        P("rep", "tp", None),
        P("rep", "tp", None, None, None),
        P("rep", "tp", None),
        P("tp", "rep", None, None),
        P("tp", "rep", None, None),
    )
    out_specs = (
        P("rep", "tp", None),
        P("rep", None, "tp"),
        P("tp", "rep", None, None),
        P("tp", "rep", None, None),
    )
    return jax.shard_map(shards, mesh=mesh, in_specs=in_specs, out_specs=out_specs, check_vma=False)
```

```python
import jax
import jax.numpy as jnp
import numpy as np
from jax import lax
from jax.experimental import pallas as pl
from jax.experimental.pallas import tpu as pltpu
from jax.sharding import PartitionSpec as P

eps = 1e-06
outer_rate = 0.7
momentum_decay = 0.9
MESH = pl.DeviceIdType.MESH
PLANES = 4
PARTS = 4
HALVES = 2
WINDOW = 7
GATHER = 5
PACK_FROM = 5
PIECES = 8
LATE = 3
EARLY = 3
AHEAD = 3
STEP_VMEM = 55 * 1024 * 1024
WRITE_FROM = pl.ANY
HEAD = 16


def dct_basis(size):
    freq = np.arange(size, dtype=np.float64)[:, None]
    place = np.arange(size, dtype=np.float64)[None, :]
    scales = np.where(freq == 0, np.sqrt(1.0 / size), np.sqrt(2.0 / size))
    return (scales * np.cos(np.pi * (2.0 * place + 1.0) * freq / (2.0 * size))).astype(np.float32)


def step_kernel(
    ids_hbm, attn_hbm, w_hbm, gain_hbm, ct_hbm, coef_hbm, tiles_hbm, mom_hbm, left_hbm, right_hbm,
    wg, ig, tiles_new, mom_new,
    attn, attn_t, w, gain, ct, coef, tiles, mom, left, right,
    part, sib_part, pair_sum, far_sum, proj, grad, acc, ig_acc,
    pack, packs_in, sums, near_out, near_in, last_out, last_in,
    ids, keys, table,
    in_sem, w_sem, attn_sem,
    core_s, core_r, z_s, z_r, gz_s, gz_r, gc_s, gc_r, gf_s, gf_r,
    pa_s, pa_r, pb_s, pb_r, ready, go,
):
    n_rep = lax.axis_size("rep")
    planes = PLANES
    n_xy = n_rep // planes
    rep, tp = lax.axis_index("rep"), lax.axis_index("tp")
    xy, zh = lax.rem(rep, n_xy), lax.div(rep, n_xy)
    core, zl = lax.rem(tp, 2), lax.div(tp, 2)
    sib = zl * 2 + 1 - core
    far = (1 - zl) * 2 + core
    diag = (1 - zl) * 2 + 1 - core
    order = (tp, far, sib, diag)
    near = zh + 1 - 2 * lax.rem(zh, 2)
    next_near = planes - 1 - zh
    width = w.shape[1]
    rows = ct.shape[0]
    s = rows // HALVES
    tile_w = tile_width(width)
    n_w = width // tile_w
    side = coef.shape[1]
    owned = tiles.shape[0]
    pairs = owned // 2
    kept = coef.shape[0]
    f32, bf16 = jnp.float32, jnp.bfloat16

    def cols(n):
        return pl.ds(pl.multiple_of(n * tile_w, tile_w), tile_w)

    def xy_peer(d):
        return zh * n_xy + lax.rem(xy + d, n_xy)

    def plane_peer(z):
        return z * n_xy + xy

    loads = []
    for h in range(HALVES):
        for p in range(PARTS):
            start = pl.multiple_of(order[p] * rows + h * s, 16)
            loads.append(pltpu.make_async_copy(
                attn_hbm.at[pl.ds(start, s)],
                attn.at[pl.ds((h * PARTS + p) * s, s)],
                attn_sem.at[h * PARTS + p],
            ))
    for copy in loads:
        copy.start()

    def w_load(n):
        return pltpu.make_async_copy(w_hbm.at[:, cols(n)], w.at[:, cols(n)], w_sem.at[n])

    for n in range(min(AHEAD, n_w)):
        w_load(n).start()

    others = [
        pltpu.make_async_copy(src, dst, in_sem.at[i])
        for i, (src, dst) in enumerate(
            ((ids_hbm, ids), (coef_hbm, coef), (ct_hbm, ct), (gain_hbm, gain), (tiles_hbm, tiles), (mom_hbm, mom),
             (left_hbm, left), (right_hbm, right))
        )
    ]
    ids_load, coef_load, ct_load, gain_load, tiles_load, mom_load, left_load, right_load = others
    ids_load.start()

    barrier = pltpu.get_barrier_semaphore()
    middle = (tp == 1) | (tp == 2)

    @pl.when(jnp.logical_not(middle))
    def _():
        for to in (sib, far):
            pl.semaphore_signal(barrier, inc=1, device_id=(rep, to), device_id_type=MESH)

    @pl.when(middle)
    def _():
        pl.semaphore_wait(barrier, 2)
        for to in (sib, far):
            pl.semaphore_signal(ready, inc=1, device_id=(rep, to), device_id_type=MESH)

    def greet_replicas():
        @pl.when(jnp.logical_not(middle))
        def _():
            pl.semaphore_wait(ready, 2)

        @pl.when(tp == 0)
        def _():
            for z in (near, next_near):
                pl.semaphore_signal(
                    barrier, inc=1, device_id=(plane_peer(z), 0), device_id_type=MESH
                )

            @pl.loop(1, n_xy)
            def _(d):
                pl.semaphore_signal(barrier, inc=1, device_id=(xy_peer(d), 0), device_id_type=MESH)

    def meet_replicas():
        @pl.when(tp == 0)
        def _():
            pl.semaphore_wait(barrier, n_xy + 1)
            for to in range(1, PARTS):
                pl.semaphore_signal(go, inc=1, device_id=(rep, to), device_id_type=MESH)

        @pl.when(tp != 0)
        def _():
            pl.semaphore_wait(go, 1)

    def remote(src, dst, send, recv, rep_to, tp_to):
        return pltpu.make_async_remote_copy(
            src_ref=src, dst_ref=dst, send_sem=send, recv_sem=recv,
            device_id=(rep_to, tp_to), device_id_type=MESH,
        )

    def make_table():
        entry = lax.broadcasted_iota(jnp.int32, (n_rep, kept), 1)
        owner = lax.broadcasted_iota(jnp.int32, (n_rep, kept), 0)
        names = jnp.broadcast_to(ids[...], (n_rep, kept))
        match = (names >= owner * owned) & (names < owner * owned + owned)
        key = entry * owned + names - owner * owned
        least = jnp.min(jnp.where(match, key, kept * owned - 1), axis=1, keepdims=True)
        most = jnp.max(jnp.where(match, key, -1), axis=1, keepdims=True)
        lane = lax.broadcasted_iota(jnp.int32, keys.shape, 1)
        keys[...] = jnp.where(lane == 0, least, most)
        table_copy().start()

    def table_copy():
        return pltpu.make_async_copy(keys, table, in_sem.at[8])

    def core_copy(h, n):
        i = h * n_w + n
        return remote(
            part.at[pl.ds((h * PARTS + 2) * s, 2 * s), cols(n)],
            sib_part.at[pl.ds(h * 2 * s, 2 * s), cols(n)],
            core_s.at[i], core_r.at[i], rep, sib,
        )

    def z_copy(h, n):
        i = h * n_w + n
        here = pl.ds(h * s, s)
        return remote(
            pair_sum.at[here, cols(n)], far_sum.at[here, cols(n)], z_s.at[i], z_r.at[i], rep, far
        )

    def grad_copy(h, n, place, to, send, recv, target):
        i = h * n_w + n
        return remote(
            grad.at[pl.ds((h * PARTS + place) * s, s), cols(n)],
            grad.at[pl.ds((h * PARTS + to) * s, s), cols(n)],
            send.at[i], recv.at[i], rep, target,
        )

    def grad_far(h, n):
        return grad_copy(h, n, 0, 1, gz_s, gz_r, far)

    def grad_core(h, n):
        return grad_copy(h, n, 0, 2, gc_s, gc_r, sib)

    def grad_forward(h, n):
        return grad_copy(h, n, 1, 3, gf_s, gf_r, sib)

    def partial_tile(h, n):
        here = slice(h * PARTS * s, (h + 1) * PARTS * s)
        part[here, cols(n)] = jnp.dot(
            attn[here, :], w[:, cols(n)], preferred_element_type=f32
        ).astype(bf16)

    def pair_tile(h, n):
        core_copy(h, n).wait_recv()
        behind(h, n, lambda a, b: z_copy(a, b).wait_send())
        base = h * PARTS * s + s
        pair_sum[h * s:h * s + s, cols(n)] = (
            part[base:base + s, cols(n)].astype(f32)
            + sib_part[h * 2 * s + s:(h + 1) * 2 * s, cols(n)].astype(f32)
        ).astype(bf16)
        z_copy(h, n).start()

    def behind(h, n, step):
        @pl.when(n >= window)
        def _():
            step(h, n - window)

        if h > 0:
            @pl.when(n < window)
            def _():
                step(h - 1, n + n_w - window)

    def ahead(h, n, step):
        @pl.when(n + gather < n_w)
        def _():
            step(h, n + gather)

        if h < HALVES - 1:
            @pl.when(n + gather >= n_w)
            def _():
                step(h + 1, n + gather - n_w)

    def fold(block):
        total = block[:, 0:128]
        for k in range(1, block.shape[1] // 128):
            total = total + block[:, k * 128:(k + 1) * 128]
        return total

    def norm_half(h):
        here = slice(h * s, h * s + s)
        base = h * PARTS * s

        def stats(n, carry):
            square, cross = carry
            z_copy(h, n).wait_recv()
            p = (
                part[base:base + s, cols(n)].astype(f32)
                + sib_part[h * 2 * s:h * 2 * s + s, cols(n)].astype(f32)
                + far_sum[here, cols(n)].astype(f32)
            )
            proj[:, cols(n)] = p
            scaled = ct[here, cols(n)].astype(f32) * gain[:, cols(n)]
            return square + fold(p * p), cross + fold(scaled * p)

        zero = jnp.zeros((s, 128), f32)
        square, cross = lax.fori_loop(0, n_w, stats, (zero, zero))
        inverse = lax.rsqrt(jnp.sum(square, axis=1, keepdims=True) / width + eps)
        slope = jnp.sum(cross, axis=1, keepdims=True) / width * inverse * inverse

        @pl.loop(0, n_w)
        def _(n):
            scaled = ct[here, cols(n)].astype(f32) * gain[:, cols(n)]
            grad[base:base + s, cols(n)] = (
                inverse * (scaled - proj[:, cols(n)] * slope)
            ).astype(bf16)
            grad_core(h, n).start()

    def send_far(h, low, high):
        @pl.loop(low, high)
        def _(n):
            grad_far(h, n).start()

    lane = lax.broadcasted_iota(jnp.int32, (HEAD, 2 * side), 1)
    line = lax.broadcasted_iota(jnp.int32, (HEAD, 2 * side), 0)

    def pack_for(d, dst):
        to = lax.rem(xy + d, n_xy)
        head = jnp.full((HEAD, 2 * side), -1.0, f32)
        for h in range(planes):
            o = h * n_xy + to
            least, most = table[o, 0], table[o, 1]
            one, two = least // owned, jnp.maximum(most, 0) // owned
            both = jnp.concatenate([coef[one], coef[two]], axis=1)
            dst[h * side:(h + 1) * side, :] = both.astype(bf16)
            one_place = jnp.where(most >= 0, least - one * owned, -1)
            two_place = jnp.where(most > least, most - two * owned, -1)
            place = jnp.where(lane < side, one_place.astype(f32), two_place.astype(f32))
            head = jnp.where(line == h, place, head)
        dst[planes * side:planes * side + HEAD, :] = head.astype(bf16)

    def pack_copy(d):
        return remote(pack.at[d], packs_in.at[d], pa_s.at[d], pa_r.at[d], xy_peer(d), tp)

    each = -(-n_xy // (n_w - 1))

    def pack_some(n):
        for i in range(each):
            d = n * each + 1 + i

            @pl.when(d < n_xy)
            def _():
                pack_for(d, pack.at[d])
                pack_copy(d).start()

            @pl.when(d == n_xy)
            def _():
                pack_for(n_xy, packs_in.at[0])

    half = lax.broadcasted_iota(jnp.int32, (1, 2 * side), 1)
    half = jnp.where(half < side, 0.0, 1.0).astype(f32)

    def near_copies(slot):
        return [
            remote(
                near_out.at[slot, pl.ds(p * side, side)], near_in.at[slot, pl.ds(p * side, side)],
                pb_s.at[slot * pairs + p], pb_r.at[slot * pairs + p], plane_peer(near), tp,
            )
            for p in range(pairs)
        ]

    def last_copies():
        return [
            remote(
                last_out.at[pl.ds(p * side, side)], last_in.at[pl.ds(p * side, side)],
                pb_s.at[2 * pairs + p], pb_r.at[2 * pairs + p], plane_peer(next_near), tp,
            )
            for p in range(pairs)
        ]

    def sum_plane(z):
        here_rows = pl.ds(pl.multiple_of(z * side, side), side)

        def add(d, totals):
            block = packs_in[d, here_rows, :].astype(f32)
            turned = pltpu.roll(block, side, 1)
            head = packs_in[d, planes * side:planes * side + HEAD, :].astype(f32)
            head = jnp.sum(jnp.where(line == z, head, 0.0), axis=0, keepdims=True)
            here = head - half
            there = pltpu.roll(jnp.broadcast_to(head, (8, 2 * side)), side, 1)[0:1, :] - half
            return tuple(
                total
                + jnp.where(here == 2.0 * p, block, 0.0)
                + jnp.where(there == 2.0 * p, turned, 0.0)
                for p, total in enumerate(totals)
            )

        zero = jnp.zeros((side, 2 * side), f32)
        return lax.fori_loop(0, n_xy, add, (zero,) * pairs)

    def sum_packs():
        @pl.loop(1, n_xy)
        def _(d):
            pack_copy(d).wait_recv()

        for slot, z in ((1, planes - 1 - near), (0, near)):
            for p, total in enumerate(sum_plane(z)):
                near_out[slot, p * side:(p + 1) * side, :] = total.astype(bf16)
            for copy in near_copies(slot):
                copy.start()
        for slot, z in ((1, next_near), (0, zh)):
            for p, total in enumerate(sum_plane(z)):
                sums[slot, p * side:(p + 1) * side, :] = total

    def pass_on():
        for copy in near_copies(1):
            copy.wait_recv()
        last_out[...] = (sums[1] + near_in[1].astype(f32)).astype(bf16)
        for copy in last_copies():
            copy.start()

    def outer_step():
        for copy in near_copies(0) + last_copies():
            copy.wait_recv()
        total = sums[0] + near_in[0].astype(f32) + last_in[...].astype(f32)
        for copy in (tiles_load, mom_load, left_load, right_load):
            copy.wait()
        wide = jnp.dot(total, right[...], precision=lax.Precision.HIGHEST)
        for p in range(pairs):
            decoded = jnp.dot(
                left[...], wide[p * side:(p + 1) * side, :], precision=lax.Precision.HIGHEST
            ) / n_rep
            for i in range(2):
                one = decoded[:, i * side:(i + 1) * side]
                fresh = momentum_decay * mom[2 * p + i] + one
                mom_new[2 * p + i] = fresh
                tiles_new[2 * p + i] = tiles[2 * p + i] - outer_rate * (one + momentum_decay * fresh)

    def arrive(h, n):
        grad_far(h, n).wait_recv()
        grad_forward(h, n).start()
        grad_far(h, n).wait_send()
        ahead(h, n, lambda a, b: grad_far(a, b).start())

    def use_tile(h, n):
        grad_core(h, n).wait_recv()
        grad_forward(h, n).wait_recv()
        here = slice(h * PARTS * s, (h + 1) * PARTS * s)
        block = grad[here, cols(n)]
        product = jnp.dot(attn_t[:, here], block, preferred_element_type=f32)
        if h == 0:
            acc[:, cols(n)] = product
        elif h < HALVES - 1:
            acc[:, cols(n)] += product
        else:
            wg[:, cols(n)] = (acc[:, cols(n)] + product).astype(bf16)
        ig_acc[here, :] += lax.dot_general(
            block, w[:, cols(n)], (((1,), (1,)), ((), ())), preferred_element_type=f32
        )

    def use_half(h, low, high):
        if low == 0:
            arrive(h, 0)

        @pl.loop(low, high)
        def _(n):
            @pl.when(n + 1 < n_w)
            def _():
                arrive(h, n + 1)

            use_tile(h, n)

    def finish_input(h):
        for p in range(PARTS):
            start = pl.multiple_of(order[p] * rows + h * s, 16)
            base = (h * PARTS + p) * s
            ig[pl.ds(start, s), :] = ig_acc[base:base + s, :].astype(bf16)

    window, gather = min(WINDOW, n_w), min(GATHER, n_w)
    pack_from = min(PACK_FROM, n_w - 1)
    for h in range(HALVES):
        for copy in loads[h * PARTS:(h + 1) * PARTS]:
            copy.wait()
        if h == 0:
            w_load(0).wait()
        partial_tile(h, 0)
        if h == 0:
            greet_replicas()
        core_copy(h, 0).start()
        if h == 0:
            for copy in others[1:]:
                copy.start()
            ids_load.wait()
            make_table()
            pair_tile(0, 0)

        @pl.loop(1, n_w)
        def _(n):
            if h == 0:
                @pl.when(n + AHEAD - 1 < n_w)
                def _():
                    w_load(n + AHEAD - 1).start()

                w_load(n).wait()
            partial_tile(h, n)
            core_copy(h, n).start()
            if h == 0:
                @pl.when(n > 1)
                def _():
                    pair_tile(h, n - 1)

                @pl.when(n == pack_from)
                def _():
                    table_copy().wait()
                    coef_load.wait()
                    meet_replicas()

                @pl.when(n >= pack_from)
                def _():
                    pack_some(n - pack_from)
            else:
                pair_tile(h, n - 1)
                if h == 1:
                    pack_some(n + n_w - 1 - pack_from)

        pair_tile(h, n_w - 1)
    attn_t[...] = attn[...].T
    ig_acc[...] = jnp.zeros_like(ig_acc)
    ct_load.wait()
    gain_load.wait()
    norm_half(0)
    send_far(0, 0, gather)
    norm_half(1)
    use_half(0, 0, EARLY)
    sum_packs()
    use_half(0, EARLY, n_w)
    finish_input(0)
    pass_on()
    use_half(1, 0, n_w - LATE)
    outer_step()
    last = n_w - LATE
    for h in range(HALVES):
        @pl.loop(0, n_w)
        def _(n):
            core_copy(h, n).wait_send()
            grad_core(h, n).wait_send()

    for h in range(HALVES):
        @pl.loop(0, n_w if h < HALVES - 1 else last)
        def _(n):
            grad_forward(h, n).wait_send()

    @pl.loop(n_w - window, n_w)
    def _(n):
        z_copy(HALVES - 1, n).wait_send()

    @pl.loop(1, n_xy)
    def _(d):
        pack_copy(d).wait_send()

    for copy in near_copies(0) + near_copies(1) + last_copies():
        copy.wait_send()
    use_half(1, last, n_w)
    finish_input(1)

    @pl.loop(last, n_w)
    def _(n):
        grad_forward(HALVES - 1, n).wait_send()


def write_kernel(*refs):
    sources, targets, sem = refs[:4], refs[4:8], refs[8]
    pieces = PIECES
    step = sources[0].shape[0] // pieces
    copies = [
        pltpu.make_async_copy(
            sources[0].at[pl.ds(i * step, step)], targets[0].at[pl.ds(i * step, step)], sem.at[i]
        )
        for i in range(pieces)
    ]
    copies += [
        pltpu.make_async_copy(sources[i], targets[i], sem.at[pieces + i - 1]) for i in range(1, 4)
    ]
    for copy in copies:
        copy.start()
    for copy in copies:
        copy.wait()


def tile_width(width):
    return 512


def shards(attn_out, proj_weight, norm_gain, cotangent, coeffs, tile_ids, tiles, momentum):
    n_rep = lax.axis_size("rep")
    attended, weights, upstream = attn_out[0], proj_weight[0], cotangent[0]
    owned, side = tiles.shape[1], tiles.shape[2]
    tokens, depth = attended.shape
    width = weights.shape[1]
    rows = upstream.shape[0]
    n_w = width // tile_width(width)
    n_xy = n_rep // PLANES
    kept = coeffs.shape[2]
    basis = dct_basis(side)
    right = np.zeros((2 * side, 2 * side), np.float32)
    right[:side, :side] = basis
    right[side:, side:] = basis
    f32, bf16 = jnp.float32, jnp.bfloat16
    dma = pltpu.SemaphoreType.DMA
    any_spec = pl.BlockSpec(memory_space=pl.ANY)
    message = PLANES * side + HEAD
    summed = owned // 2 * side
    results = (
        ((depth, width), bf16),
        ((tokens, depth), bf16),
        ((owned, side, side), f32),
        ((owned, side, side), f32),
    )
    operands = (
        tile_ids[0], attended, weights, norm_gain, upstream, coeffs[0, 0], tiles[0], momentum[0],
        jnp.asarray(np.ascontiguousarray(basis.T)), jnp.asarray(right),
    )
    held = pl.pallas_call(
        step_kernel,
        out_shape=tuple(pltpu.VMEM(shape, dtype) for shape, dtype in results),
        in_specs=[any_spec] * len(operands),
        out_specs=(pl.BlockSpec(memory_space=pltpu.VMEM),) * 4,
        scratch_shapes=[
            pltpu.VMEM((tokens, depth), bf16),
            pltpu.VMEM((depth, tokens), bf16),
            pltpu.VMEM((depth, width), bf16),
            pltpu.VMEM((1, width), f32),
            pltpu.VMEM((rows, width), bf16),
            pltpu.VMEM((kept, side, side), f32),
            pltpu.VMEM((owned, side, side), f32),
            pltpu.VMEM((owned, side, side), f32),
            pltpu.VMEM((side, side), f32),
            pltpu.VMEM((2 * side, 2 * side), f32),
            pltpu.VMEM((tokens, width), bf16),
            pltpu.VMEM((2 * rows, width), bf16),
            pltpu.VMEM((rows, width), bf16),
            pltpu.VMEM((rows, width), bf16),
            pltpu.VMEM((rows // HALVES, width), f32),
            pltpu.VMEM((tokens, width), bf16),
            pltpu.VMEM((depth, width), f32),
            pltpu.VMEM((tokens, depth), f32),
            pltpu.VMEM((n_xy, message, 2 * side), bf16),
            pltpu.VMEM((n_xy, message, 2 * side), bf16),
            pltpu.VMEM((2, summed, 2 * side), f32),
            pltpu.VMEM((2, summed, 2 * side), bf16),
            pltpu.VMEM((2, summed, 2 * side), bf16),
            pltpu.VMEM((summed, 2 * side), bf16),
            pltpu.VMEM((summed, 2 * side), bf16),
            pltpu.VMEM((1, kept), jnp.int32),
            pltpu.VMEM((n_rep, 128), jnp.int32),
            pltpu.SMEM((n_rep, 128), jnp.int32),
            dma((9,)), dma((n_w,)), dma((HALVES * PARTS,)),
            *[dma((HALVES * n_w,)) for _ in range(10)],
            dma((n_xy,)), dma((n_xy,)), dma((3 * (owned // 2),)), dma((3 * (owned // 2),)),
            pltpu.SemaphoreType.REGULAR, pltpu.SemaphoreType.REGULAR,
        ],
        compiler_params=pltpu.CompilerParams(
            collective_id=0, has_side_effects=True, vmem_limit_bytes=STEP_VMEM
        ),
        cost_estimate=pl.CostEstimate(
            flops=6 * tokens * depth * width, bytes_accessed=16_000_000, transcendentals=0
        ),
    )(*operands)
    outs = pl.pallas_call(
        write_kernel,
        out_shape=tuple(jax.ShapeDtypeStruct(shape, dtype) for shape, dtype in results),
        in_specs=[pl.BlockSpec(memory_space=WRITE_FROM)] * 4,
        out_specs=(any_spec,) * 4,
        scratch_shapes=[dma((PIECES + 3,))],
        compiler_params=pltpu.CompilerParams(vmem_limit_bytes=4 * 1024 * 1024),
    )(*held)
    return tuple(out[None] for out in outs)


def solution(mesh):
    in_specs = (
        P("rep", None, "tp"),
        P("rep", "tp", None),
        P("rep", None),
        P("rep", "tp", None),
        P("rep", "tp", None, None, None),
        P("rep", "tp", None),
        P("tp", "rep", None, None),
        P("tp", "rep", None, None),
    )
    out_specs = (
        P("rep", "tp", None),
        P("rep", None, "tp"),
        P("tp", "rep", None, None),
        P("tp", "rep", None, None),
    )
    return jax.shard_map(shards, mesh=mesh, in_specs=in_specs, out_specs=out_specs, check_vma=False)
```
